128 devices in a mesh: wave: 8 (over y_hi, x), row: 16 (over y_lo, z, core).
Axes of the slice: x: 4, y: 4 (y_hi: 2, y_lo: 2; y = y_hi * 2 + y_lo), z: 4, core: 2. Of those that a mesh axis runs over, the one named last changes fastest.
Arguments:
- plane_waves: float32 [2, 8, 2048, 2048], P(None, 'wave', 'row'), may hold values from -6 to 6
- transmission: float32 [1, 2, 2048, 2048], P(None, None, 'row')
- wave_index: int32 [8, 2], P('wave'), may hold values from -32 to 31
- wave_weight: float32 [8], P('wave'), may hold values from 0.3 to 3
- wave_phase: float32 [8], P('wave'), may hold values from -3.140625 to 3.140625
- probe_pos: int32 [128, 2], replicated, may hold values from 0 to 2047, as said below
Outputs:
- diffraction: float32 [128, 128, 128], P('row', 'wave')
The draws below stay inside these ranges and needn't reach their ends.
Inputs may be any that keep to these rules, and one draw needn't show every extreme that they name: `probe_pos`: the probes numbered j * 8 to (j + 1) * 8 - 1 have their grid row (first entry) in j * 128 to (j + 1) * 128 - 1; the second entry is the grid column.
All inputs are finite; a program needn't handle non-finite values.
Results may differ from the reference program's by a relative error of at most 0.0003.
Values sent between devices are 32-bit elements; how exact they have to be, the bound alone decides.
A program may use at most 64 MiB of HBM per device.

```python
import math
import jax
import jax.numpy as jnp
from jax import lax

GRID = 2048
FACTOR = 16
WINDOW = 128
HALF = 64
SLICES = 1
WAVES = 8
ROWS_DEV = 128
PROBES_DEV = 8
PROBES = 128


def draw_transmission(key, part):
    key_amp, key_shift = jax.random.split(key)
    amplitude = jax.random.uniform(key_amp, (SLICES, GRID, GRID), jnp.float32, 0.75, 1.0)
    phase_shift = jax.random.uniform(key_shift, (SLICES, GRID, GRID), jnp.float32, -1.2, 1.2)
    return jnp.stack((amplitude * jnp.cos(phase_shift), amplitude * jnp.sin(phase_shift)), axis=1)


def draw_probe_pos(key, part):
    subkeys = jax.random.split(key, 4)
    block_count = PROBES // PROBES_DEV
    numbers = jnp.arange(PROBES, dtype=jnp.int32)
    owner_block = numbers // PROBES_DEV
    within = numbers % PROBES_DEV
    grid_rows = owner_block * ROWS_DEV + jax.random.randint(subkeys[0], (PROBES,), 0, ROWS_DEV, dtype=jnp.int32)
    grid_cols = jax.random.randint(subkeys[1], (PROBES,), 0, GRID, dtype=jnp.int32)
    first_slot = jax.random.randint(subkeys[2], (block_count,), 0, PROBES_DEV, dtype=jnp.int32)
    second_slot = (first_slot + 1 + jax.random.randint(subkeys[3], (block_count,), 0, PROBES_DEV - 1, dtype=jnp.int32)) % PROBES_DEV
    is_first = within == first_slot[owner_block]
    is_second = within == second_slot[owner_block]
    grid_rows = jnp.where(is_first, owner_block * ROWS_DEV, grid_rows)
    grid_rows = jnp.where(is_second, owner_block * ROWS_DEV + ROWS_DEV - 1, grid_rows)
    grid_cols = jnp.where(is_first, 0, grid_cols)
    grid_cols = jnp.where(is_second, GRID - 1, grid_cols)
    return jnp.stack((grid_rows, grid_cols), axis=1)


def plant(values, own_key, smallest, high):
    place = [jax.random.randint(jax.random.fold_in(own_key, axis), (), 0, length) for axis, length in enumerate(values.shape)]
    longest = values.shape.index(max(values.shape))
    neighbour = place[:longest] + [(place[longest] + 1) % values.shape[longest]] + place[longest + 1:]
    return values.at[tuple(place)].set(smallest).at[tuple(neighbour)].set(high)


def shard_levels(key, dims, cuts, low, high):
    factor_of = 1.0
    for dim, parts in cuts:
        steps = jax.random.uniform(jax.random.fold_in(jax.random.fold_in(key, 6), dim), (parts,), jnp.float32, low / len(cuts), high / len(cuts))
        factor_of = factor_of * jnp.repeat(jnp.exp(steps), dims[dim] // parts).reshape((-1,) + (1,) * (len(dims) - 1 - dim))
    return factor_of


def gaussian(rng, shape, spread, bound, cuts=(), held_as=jnp.bfloat16):
    values = jax.random.normal(rng, shape, jnp.float32) * spread
    if len(cuts) > 0:
        values = shard_levels(rng, shape, cuts, -0.22, 0.18) * values
    return jnp.clip(values, min=-bound, max=bound).astype(held_as)


def setup_inputs(seed: int = 0) -> dict:
    streams_of = jax.random.split(jax.random.key(seed), 7)
    return {
        "plane_waves": gaussian(streams_of[0], (2, WAVES, GRID, GRID), 1.0, 6.0, ((1, 8), (2, 16)), jnp.float32),
        "transmission": draw_transmission(jax.random.fold_in(streams_of[6], 71), 0),
        "wave_index": plant(jax.random.randint(streams_of[2], (WAVES, 2), -(WINDOW // 4), WINDOW // 4), jax.random.fold_in(streams_of[2], 1), -(WINDOW // 4), (WINDOW // 4) - 1).astype(jnp.int32),
        "wave_weight": jnp.clip(jnp.exp(math.log(3.0) - 2.3025851 * jax.random.uniform(streams_of[3], (WAVES,), jnp.float32) ** shard_levels(streams_of[3], (WAVES,), ((0, 8),), -0.2, 0.2)), 0.3, 3.0),
        "wave_phase": jnp.clip(jax.random.uniform(streams_of[4], (WAVES,), jnp.float32, -3.140625, 3.140625), -3.140625, 3.140625),
        "probe_pos": draw_probe_pos(jax.random.fold_in(streams_of[6], 71), 0),
    }


FRESNEL = 0.1
EXACT_PRECISION = lax.Precision.HIGHEST


def propagator_parts():
    indices = jnp.arange(GRID, dtype=jnp.int32)
    frequency = jnp.where(indices < GRID // 2, indices, indices - GRID)
    radius = frequency[:, None] * frequency[:, None] + frequency[None, :] * frequency[None, :]
    phase_angle = radius.astype(jnp.float32) * (math.pi * FRESNEL / GRID)
    inside = 9 * radius <= GRID * GRID
    return jnp.where(inside, jnp.cos(phase_angle), 0.0), jnp.where(inside, -jnp.sin(phase_angle), 0.0)


def coefficients(positions, wave_index, wave_weight, wave_phase):
    grid_rows = positions[:, 0:1]
    grid_cols = positions[:, 1:2]
    turns = (FACTOR * (grid_rows * wave_index[None, :, 0] + grid_cols * wave_index[None, :, 1])) % GRID
    angles = wave_phase[None, :] - turns.astype(jnp.float32) * (2.0 * math.pi / GRID)
    return wave_weight[None, :] * jnp.cos(angles), wave_weight[None, :] * jnp.sin(angles)


def reference(plane_waves, transmission, wave_index, wave_weight, wave_phase, probe_pos):
    prop_re, prop_im = propagator_parts()
    propagator = lax.complex(prop_re, prop_im)
    layers = lax.complex(transmission[:, 0], transmission[:, 1])

    def advance(halves):
        field = lax.complex(halves[0], halves[1])
        for slice_index in range(SLICES):
            field = field * layers[slice_index]
            field = jnp.fft.ifft2(propagator * jnp.fft.fft2(field))
        return jnp.real(field), jnp.imag(field)

    exit_re, exit_im = lax.map(advance, (plane_waves[0], plane_waves[1]))
    padded = jnp.pad(jnp.stack((exit_re, exit_im)), ((0, 0), (0, 0), (HALF, HALF), (HALF, HALF)), mode="wrap")
    coef_re, coef_im = coefficients(probe_pos, wave_index, wave_weight, wave_phase)

    def probe_image(item):
        row_start, col_start, weight_re, weight_im = item
        zero_index = jnp.zeros((), jnp.int32)
        window_cut = lax.dynamic_slice(padded, (zero_index, zero_index, row_start.astype(jnp.int32), col_start.astype(jnp.int32)), (2, WAVES, WINDOW, WINDOW))
        real_part = jnp.einsum("w,wij->ij", weight_re, window_cut[0], precision=EXACT_PRECISION) - jnp.einsum("w,wij->ij", weight_im, window_cut[1], precision=EXACT_PRECISION)
        imag_part = jnp.einsum("w,wij->ij", weight_re, window_cut[1], precision=EXACT_PRECISION) + jnp.einsum("w,wij->ij", weight_im, window_cut[0], precision=EXACT_PRECISION)
        spectrum = jnp.fft.fft2(lax.complex(real_part, imag_part))
        spec_re = jnp.real(spectrum)
        spec_im = jnp.imag(spectrum)
        return (spec_re * spec_re + spec_im * spec_im) / (WINDOW * WINDOW * WAVES)

    return lax.map(probe_image, (probe_pos[:, 0], probe_pos[:, 1], coef_re, coef_im))
```

```python
import functools
import math

import jax
import jax.numpy as jnp
import ml_dtypes
import numpy as np
from jax import lax
from jax.experimental import pallas as pl
from jax.experimental.pallas import tpu as pltpu
from jax.sharding import PartitionSpec as P

MESH = pl.DeviceIdType.MESH
F32 = jnp.float32
BF16 = jnp.bfloat16

GRID = 2048
PARTS = 16
LANES = 128
WINDOW = 128
HALF = 64
FACTOR = 16
FRESNEL = 0.1
GROUPS = 11
KEEP = 8 * GROUPS
FIRST = -KEEP // 2
BLOCK = 2 * KEEP
DEPTH = PARTS * BLOCK
CHUNKS = ((0, 5), (5, 9), (9, 11))
PROBES = 8
NT = (((1,), (1,)), ((), ()))


def split_host(table):
    table = np.asarray(table, np.float32)
    high = table.astype(ml_dtypes.bfloat16)
    low = (table - high.astype(np.float32)).astype(ml_dtypes.bfloat16)
    return high, low


def host_tables(wave_count):
    lane = np.arange(LANES)
    freq = np.arange(KEEP) + FIRST
    group, part, member = np.meshgrid(np.arange(GROUPS), np.arange(2), np.arange(8), indexing="ij")
    row_freq = (group * 8 + member).reshape(-1) + FIRST
    row_imag = part.reshape(-1)

    angle = 2 * math.pi * (row_freq[:, None] * lane[None, :] % LANES) / LANES
    imag = row_imag[:, None] == 1
    forward_x = np.concatenate(
        [np.where(imag, -np.sin(angle), np.cos(angle)), np.where(imag, np.cos(angle), np.sin(angle))], axis=1
    )
    high, low = split_host(forward_x)
    forward_x = np.concatenate([high, high, low], axis=1)

    angle = 2 * math.pi * (lane[:, None] * freq[None, :] % LANES) / LANES
    pad = np.zeros((LANES, LANES - KEEP))
    cos = np.concatenate([np.cos(angle), pad], axis=1)
    sin = np.concatenate([np.sin(angle), pad], axis=1)
    forward_y = np.block([[cos, -sin], [sin, cos]])
    inverse_y = np.block([[cos.T, sin.T], [-sin.T, cos.T]])
    high, low = split_host(forward_y)
    forward_y = np.concatenate([high, high, low], axis=0)
    high, low = split_host(inverse_y)
    inverse_y = np.concatenate([high, high, low], axis=0)

    k1 = np.arange(PARTS)
    angle = -2 * math.pi * (k1[:, None] * lane[None, :]) / GRID
    twiddle = np.stack([np.cos(angle), np.sin(angle)], axis=1).astype(np.float32)
    twiddle = np.ascontiguousarray(np.broadcast_to(twiddle[:, :, None, :], (PARTS, 2, 8, LANES)))

    ky = k1[:, None] + 16 * np.concatenate([freq, np.full(LANES - KEEP, 4 * GRID)])[None, :]
    angle = -math.pi * FRESNEL / GRID * (ky.astype(np.float64) ** 2) - 2 * math.pi * (HALF * ky % GRID) / GRID
    inside = np.abs(ky) < GRID
    scale = inside / float(GRID * GRID)
    prop = np.stack([scale * np.cos(angle), scale * np.sin(angle)], axis=1).astype(np.float32)
    nine = np.where(inside, 9 * ky * ky, 2**30).astype(np.int32)[:, None, :]

    depth_kx, depth_imag = [], []
    for begin, end in CHUNKS:
        for source in range(PARTS):
            rows = slice(16 * begin, 16 * end)
            depth_kx.append(source + 16 * row_freq[rows])
            depth_imag.append(row_imag[rows])
    depth_kx = np.concatenate(depth_kx)
    depth_imag = np.concatenate(depth_imag)
    order = np.arange(WINDOW)
    mu = depth_kx[None, :] - 16 * order[:, None]
    dirichlet = np.zeros(mu.shape)
    for m in range(WINDOW // 2):
        dirichlet += 2 * np.cos(math.pi * ((2 * m + 1) * mu % (2 * GRID)) / GRID)
    dirichlet = dirichlet.astype(np.float32)
    fresnel = -math.pi * FRESNEL / GRID * depth_kx.astype(np.float64) ** 2
    fresnel = np.mod(fresnel + math.pi, 2 * math.pi) - math.pi
    phase_f = fresnel.astype(np.float32)[None, :]
    phase_i = np.stack([depth_kx, 1024 * depth_imag]).astype(np.int32)

    share = WINDOW // wave_count
    s, ri, q = np.meshgrid(np.arange(wave_count), np.arange(2), np.arange(share), indexing="ij")
    out_q = (s * share + q).reshape(-1)
    imag = ri.reshape(-1)[:, None] == 1
    angle = 2 * math.pi * (out_q[:, None] * lane[None, :] % LANES) / LANES
    last = np.concatenate(
        [np.where(imag, -np.sin(angle), np.cos(angle)), np.where(imag, np.cos(angle), np.sin(angle))], axis=1
    )
    high, low = split_host(last)
    last = np.concatenate([high, high, low], axis=1)
    return (forward_x, forward_y, inverse_y, twiddle, prop, nine, dirichlet, phase_f, phase_i, last)


def split(x):
    high = x.astype(BF16)
    low = (x - high.astype(F32)).astype(BF16)
    return high, low


def four(values, sign):
    (ar, ai), (br, bi), (cr, ci), (dr, di) = values
    s0r, s0i, s1r, s1i = ar + cr, ai + ci, ar - cr, ai - ci
    s2r, s2i, s3r, s3i = br + dr, bi + di, br - dr, bi - di
    if sign < 0:
        s3r, s3i = s3i, -s3r
        return [(s0r + s2r, s0i + s2i), (s1r + s3r, s1i + s3i), (s0r - s2r, s0i - s2i), (s1r - s3r, s1i - s3i)]
    return [(s0r + s2r, s0i + s2i), (s1r - s3i, s1i + s3r), (s0r - s2r, s0i - s2i), (s1r + s3i, s1i - s3r)]


def turn(value, power, sign):
    re, im = value
    power = power % 16
    if power == 0:
        return value
    if power == 4:
        return (im, -re) if sign < 0 else (-im, re)
    half = math.sqrt(0.5)
    if power == 2:
        if sign < 0:
            return (re + im) * half, (im - re) * half
        return (re - im) * half, (im + re) * half
    if power == 6:
        if sign < 0:
            return (im - re) * half, (re + im) * -half
        return (re + im) * -half, (re - im) * half
    c, s = math.cos(2 * math.pi * power / 16), sign * math.sin(2 * math.pi * power / 16)
    return re * c - im * s, re * s + im * c


def sixteen(values, sign):
    inner = [four([values[4 * a1 + a0] for a1 in range(4)], sign) for a0 in range(4)]
    out = [None] * 16
    for k0 in range(4):
        column = four([turn(inner[a0][k0], a0 * k0, sign) for a0 in range(4)], sign)
        for k1 in range(4):
            out[k0 + 4 * k1] = column[k1]
    return out


def cmul(ar, ai, br, bi):
    return ar * br - ai * bi, ar * bi + ai * br


def body(
    wave_count,
    pw_hbm, tr_hbm, fx_hbm, fy_hbm, iy_hbm, tw_hbm, py_hbm, nine_hbm, dk_hbm, pf_hbm, pi_hbm, last_hbm,
    pos_vec, pos_s, windex, wweight, wphase,
    out_ref,
    pw, tr, fx, fy, iy, tw, py, nine, dk, pf, pi, last,
    yx, send1, recv1, yy, send2, recv2, rows_re, rows_im, a_hi, a_lo, total, send3, recv3,
    load_sem, send1_sem, recv1_sem, send2_sem, recv2_sem, local_sem, send3_sem, recv3_sem,
):
    me = lax.axis_index("row")
    wv = lax.axis_index("wave")
    share = WINDOW // wave_count

    barrier = pltpu.get_barrier_semaphore()

    def greet_row(d, _):
        pl.semaphore_signal(barrier, inc=1, device_id={"row": lax.rem(me + d, PARTS)}, device_id_type=MESH)
        return 0

    def greet_wave(d, _):
        pl.semaphore_signal(barrier, inc=1, device_id={"wave": lax.rem(wv + d, wave_count)}, device_id_type=MESH)
        return 0

    lax.fori_loop(1, PARTS, greet_row, 0)
    if wave_count > 1:
        lax.fori_loop(1, wave_count, greet_wave, 0)

    tables = ((fx_hbm, fx), (tw_hbm, tw), (dk_hbm, dk), (pf_hbm, pf), (pi_hbm, pi), (fy_hbm, fy), (iy_hbm, iy),
              (py_hbm, py), (nine_hbm, nine), (last_hbm, last))
    loads = [pltpu.make_async_copy(pw_hbm.at[:, 0], pw, load_sem.at[0]),
             pltpu.make_async_copy(tr_hbm.at[0], tr, load_sem.at[1])]
    loads += [pltpu.make_async_copy(src, dst, load_sem.at[2 + n]) for n, (src, dst) in enumerate(tables)]
    for load in loads:
        load.start()
    for load in loads[:4]:
        load.wait()

    with jax.named_scope("column_transform"):
        def columns_16(r, _):
            rows = pl.ds(pl.multiple_of(r * 8, 8), 8)
            values = []
            for a in range(PARTS):
                cols = slice(a * LANES, (a + 1) * LANES)
                values.append(cmul(pw[0, rows, cols], pw[1, rows, cols], tr[0, rows, cols], tr[1, rows, cols]))
            for k, (re, im) in enumerate(sixteen(values, -1)):
                if k > 0:
                    re, im = cmul(re, im, tw[k, 0], tw[k, 1])
                yx[k, rows, :LANES] = re
                yx[k, rows, LANES:] = im
            return 0

        lax.fori_loop(0, LANES // 8, columns_16, 0)

    pl.semaphore_wait(barrier, PARTS - 1 + wave_count - 1)

    def copy1(c, peer):
        begin, end = CHUNKS[c]
        rows = pl.ds(16 * begin, 16 * (end - begin))
        return pltpu.make_async_remote_copy(
            src_ref=send1.at[peer, rows], dst_ref=recv1.at[me, rows],
            send_sem=send1_sem.at[c, peer], recv_sem=recv1_sem.at[c, me],
            device_id={"row": peer}, device_id_type=MESH,
        )

    def arrived1(c, source):
        begin, end = CHUNKS[c]
        rows = pl.ds(16 * begin, 16 * (end - begin))
        return pltpu.make_async_remote_copy(
            src_ref=send1.at[source, rows], dst_ref=recv1.at[source, rows],
            send_sem=send1_sem.at[c, source], recv_sem=recv1_sem.at[c, source],
            device_id={"row": source}, device_id_type=MESH,
        )

    with jax.named_scope("column_products"):
        def product(j):
            high, low = split(yx[j])
            return lax.dot_general(
                fx[...], jnp.concatenate([high, low, high], axis=1), NT, preferred_element_type=F32
            )

        def columns_128(d, _):
            j = lax.rem(me + d, PARTS)
            send1[j] = product(j)
            copy1(0, j).start()
            return 0

        lax.fori_loop(1, PARTS, columns_128, 0)
        for c in range(1, len(CHUNKS)):
            def more(d, _):
                copy1(c, lax.rem(me + d, PARTS)).start()
                return 0

            lax.fori_loop(1, PARTS, more, 0)
        recv1[me] = product(me)

    with jax.named_scope("window_weights"):
        for load in loads[4:]:
            load.wait()
        pos = pos_vec[pl.ds(pl.multiple_of(me * PROBES, PROBES), PROBES), :]
        r0, c0 = pos[:, 0:1], pos[:, 1:2]
        tilt = FACTOR * (r0 * windex[0, 0] + c0 * windex[0, 1])
        units = (2 * (c0 - HALF) + (WINDOW - 1)) * pi[0:1, :] + pi[1:2, :] - 2 * tilt
        units = jnp.bitwise_and(units, 2 * GRID - 1)
        angle = units.astype(F32) * (math.pi / GRID) + pf[...] + wphase[0]
        rows_re[...] = jnp.cos(angle) * wweight[0]
        rows_im[...] = jnp.sin(angle) * wweight[0]

        def weights_of(n, _):
            p, part = n // 8, lax.rem(n, 8)
            rows = pl.ds(pl.multiple_of(part * 16, 16), 16)
            rows2 = pl.ds(pl.multiple_of(part * 16 + WINDOW, 16), 16)
            base = dk[rows, :]
            high, low = split(base * rows_re[pl.ds(p, 1), :])
            a_hi[p, rows, :] = high
            a_lo[p, rows, :] = low
            high, low = split(base * rows_im[pl.ds(p, 1), :])
            a_hi[p, rows2, :] = high
            a_lo[p, rows2, :] = low
            return 0

        lax.fori_loop(0, PROBES * 8, weights_of, 0)

    def slot2(c, source):
        begin, end = CHUNKS[c]
        size = 16 * (end - begin)
        return pl.ds(pl.multiple_of(256 * begin + source * size, 16), size)

    def copy2(c, which, peer):
        begin, end = CHUNKS[c]
        rows = pl.ds(16 * begin, 16 * (end - begin))
        return pltpu.make_async_remote_copy(
            src_ref=send2.at[lax.rem(peer + which, PARTS), rows], dst_ref=recv2.at[which, slot2(c, me)],
            send_sem=send2_sem.at[c, which, peer], recv_sem=recv2_sem.at[c, which, me],
            device_id={"row": peer}, device_id_type=MESH,
        )

    def arrived2(c, which, source):
        begin, end = CHUNKS[c]
        rows = pl.ds(16 * begin, 16 * (end - begin))
        return pltpu.make_async_remote_copy(
            src_ref=send2.at[source, rows], dst_ref=recv2.at[which, slot2(c, source)],
            send_sem=send2_sem.at[c, which, source], recv_sem=recv2_sem.at[c, which, source],
            device_id={"row": source}, device_id_type=MESH,
        )

    def keep2(c, which):
        begin, end = CHUNKS[c]
        rows = pl.ds(16 * begin, 16 * (end - begin))
        return pltpu.make_async_copy(
            send2.at[lax.rem(me + which, PARTS), rows], recv2.at[which, slot2(c, me)], local_sem.at[c, which]
        )

    for c, (begin, end) in enumerate(CHUNKS):
        size = 8 * (end - begin)
        with jax.named_scope("wait_columns"):
            def wait1(d, _):
                arrived1(c, lax.rem(me + PARTS - d, PARTS)).wait_recv()
                return 0

            lax.fori_loop(1, PARTS, wait1, 0)

        with jax.named_scope("row_transform"):
            def rows_16(g, _):
                re_rows = pl.ds(pl.multiple_of(g * 16, 8), 8)
                im_rows = pl.ds(pl.multiple_of(g * 16 + 8, 8), 8)
                here = pl.ds(pl.multiple_of((g - begin) * 8, 8), 8)
                values = [(recv1[a, re_rows, :], recv1[a, im_rows, :]) for a in range(PARTS)]
                for k, (re, im) in enumerate(sixteen(values, -1)):
                    if k > 0:
                        re, im = cmul(re, im, tw[k, 0], tw[k, 1])
                    yy[k, here, :LANES] = re
                    yy[k, here, LANES:] = im
                return 0

            lax.fori_loop(begin, end, rows_16, 0)

            kx = me + 16 * (FIRST + 8 * begin + lax.broadcasted_iota(jnp.int32, (1, size, LANES), 1))
            limit = GRID * GRID - 9 * kx * kx

            def products(n, _):
                ks = pl.ds(n * 4, 4)
                y = yy[ks, :size, :].reshape(4 * size, 2 * LANES)
                high, low = split(y)
                f = jnp.dot(jnp.concatenate([high, low, high], axis=1), fy[...], preferred_element_type=F32)
                f = f.reshape(4, size, 2 * LANES)
                re, im = cmul(f[:, :, :LANES], f[:, :, LANES:], py[ks, 0:1, :], py[ks, 1:2, :])
                open_ = nine[ks] <= limit
                re = jnp.where(open_, re, 0.0)
                im = jnp.where(open_, im, 0.0)
                f = jnp.concatenate([re, im], axis=2).reshape(4 * size, 2 * LANES)
                high, low = split(f)
                f = jnp.dot(jnp.concatenate([high, low, high], axis=1), iy[...], preferred_element_type=F32)
                yy[ks, :size, :] = f.reshape(4, size, 2 * LANES)
                return 0

            lax.fori_loop(0, 4, products, 0)

            def rows_back(g, _):
                re_rows = pl.ds(pl.multiple_of(g * 16, 8), 8)
                im_rows = pl.ds(pl.multiple_of(g * 16 + 8, 8), 8)
                here = pl.ds(pl.multiple_of((g - begin) * 8, 8), 8)
                values = []
                for k in range(PARTS):
                    re, im = yy[k, here, :LANES], yy[k, here, LANES:]
                    if k > 0:
                        re, im = cmul(re, im, tw[k, 0], -tw[k, 1])
                    values.append((re, im))
                for a, (re, im) in enumerate(sixteen(values, 1)):
                    send2[a, re_rows, :] = re
                    send2[a, im_rows, :] = im
                return 0

            lax.fori_loop(begin, end, rows_back, 0)

        with jax.named_scope("send_rows"):
            def send(d, _):
                peer = lax.rem(me + d, PARTS)
                copy2(c, 0, peer).start()
                copy2(c, 1, peer).start()
                return 0

            lax.fori_loop(1, PARTS, send, 0)
            keep2(c, 0).start()
            keep2(c, 1).start()

    for c, (begin, end) in enumerate(CHUNKS):
        with jax.named_scope("wait_rows"):
            keep2(c, 0).wait()
            keep2(c, 1).wait()

            def wait2(d, _):
                source = lax.rem(me + PARTS - d, PARTS)
                arrived2(c, 0, source).wait_recv()
                arrived2(c, 1, source).wait_recv()
                return 0

            lax.fori_loop(1, PARTS, wait2, 0)
        with jax.named_scope("window_columns"):
            deep = slice(256 * begin, 256 * end)
            y = jnp.concatenate([recv2[0, deep, :], recv2[1, deep, :]], axis=1)
            high, low = split(y)

            def contract(p, _):
                t = jnp.dot(a_hi[p, :, deep], high, preferred_element_type=F32)
                t += jnp.dot(a_hi[p, :, deep], low, preferred_element_type=F32)
                t += jnp.dot(a_lo[p, :, deep], high, preferred_element_type=F32)
                if c == 0:
                    total[p] = t
                else:
                    total[p] += t
                return 0

            lax.fori_loop(0, PROBES, contract, 0)

    with jax.named_scope("window_rows"):
        lane = lax.broadcasted_iota(jnp.int32, (1, LANES), 1)

        def finish(p, _):
            offset = pos_s[me * PROBES + p, 0] - me * LANES
            t = total[p]
            u = jnp.where(lane >= offset, t[:, :LANES], t[:, LANES:])
            u = jnp.concatenate([u[:WINDOW], u[WINDOW:]], axis=1)
            high, low = split(u)
            v = lax.dot_general(
                last[...], jnp.concatenate([high, low, high], axis=1), NT, preferred_element_type=F32
            )
            send3[:, p] = v.reshape(wave_count, 2 * share, LANES)
            return 0

        lax.fori_loop(0, PROBES, finish, 0)

    with jax.named_scope("add_waves"):
        def copy3(peer, slot):
            return pltpu.make_async_remote_copy(
                src_ref=send3.at[peer], dst_ref=recv3.at[slot],
                send_sem=send3_sem.at[peer], recv_sem=recv3_sem.at[slot],
                device_id={"wave": peer}, device_id_type=MESH,
            )

        if wave_count > 1:
            def send_sum(d, _):
                copy3(lax.rem(wv + d, wave_count), wv).start()
                return 0

            lax.fori_loop(1, wave_count, send_sum, 0)
        recv3[wv] = send3[wv]
        if wave_count > 1:
            def wait3(d, _):
                source = lax.rem(wv + wave_count - d, wave_count)
                copy3(source, source).wait_recv()
                return 0

            lax.fori_loop(1, wave_count, wait3, 0)

        def intensity(p, _):
            v = recv3[0, p]
            for w in range(1, wave_count):
                v = v + recv3[w, p]
            re, im = v[:share], v[share:]
            out_ref[p] = (re * re + im * im) * (1.0 / (WINDOW * WINDOW * wave_count))
            return 0

        lax.fori_loop(0, PROBES, intensity, 0)

    with jax.named_scope("drain"):
        def drain(d, _):
            peer = lax.rem(me + d, PARTS)
            for c in range(len(CHUNKS)):
                copy1(c, peer).wait_send()
                copy2(c, 0, peer).wait_send()
                copy2(c, 1, peer).wait_send()
            return 0

        lax.fori_loop(1, PARTS, drain, 0)
        if wave_count > 1:
            def drain3(d, _):
                copy3(lax.rem(wv + d, wave_count), wv).wait_send()
                return 0

            lax.fori_loop(1, wave_count, drain3, 0)


def shards(wave_count, plane_waves, transmission, wave_index, wave_weight, wave_phase, probe_pos):
    tables = [jnp.asarray(t) for t in host_tables(wave_count)]
    share = WINDOW // wave_count
    rows = plane_waves.shape[2]
    chunks = len(CHUNKS)
    largest = max(8 * (end - begin) for begin, end in CHUNKS)
    any_ = pl.BlockSpec(memory_space=pl.ANY)
    vmem = pl.BlockSpec(memory_space=pltpu.VMEM)
    smem = pl.BlockSpec(memory_space=pltpu.SMEM)
    return pl.pallas_call(
        functools.partial(body, wave_count),
        out_shape=jax.ShapeDtypeStruct((PROBES, share, LANES), F32),
        in_specs=[any_] * 12 + [vmem] + [smem] * 4,
        out_specs=vmem,
        scratch_shapes=[
            pltpu.VMEM((2, rows, GRID), F32),
            pltpu.VMEM((2, rows, GRID), F32),
        ]
        + [pltpu.VMEM(t.shape, t.dtype) for t in tables]
        + [
            pltpu.VMEM((PARTS, LANES, 2 * LANES), F32),
            pltpu.VMEM((PARTS, BLOCK, LANES), F32),
            pltpu.VMEM((PARTS, BLOCK, LANES), F32),
            pltpu.VMEM((PARTS, largest, 2 * LANES), F32),
            pltpu.VMEM((PARTS, BLOCK, LANES), F32),
            pltpu.VMEM((2, DEPTH, LANES), F32),
            pltpu.VMEM((PROBES, DEPTH), F32),
            pltpu.VMEM((PROBES, DEPTH), F32),
            pltpu.VMEM((PROBES, 2 * WINDOW, DEPTH), BF16),
            pltpu.VMEM((PROBES, 2 * WINDOW, DEPTH), BF16),
            pltpu.VMEM((PROBES, 2 * WINDOW, 2 * LANES), F32),
            pltpu.VMEM((wave_count, PROBES, 2 * share, LANES), F32),
            pltpu.VMEM((wave_count, PROBES, 2 * share, LANES), F32),
            pltpu.SemaphoreType.DMA((2 + len(tables),)),
            pltpu.SemaphoreType.DMA((chunks, PARTS)),
            pltpu.SemaphoreType.DMA((chunks, PARTS)),
            pltpu.SemaphoreType.DMA((chunks, 2, PARTS)),
            pltpu.SemaphoreType.DMA((chunks, 2, PARTS)),
            pltpu.SemaphoreType.DMA((chunks, 2)),
            pltpu.SemaphoreType.DMA((wave_count,)),
            pltpu.SemaphoreType.DMA((wave_count,)),
        ],
        compiler_params=pltpu.CompilerParams(
            collective_id=0, has_side_effects=True, vmem_limit_bytes=60 * 1024 * 1024
        ),
    )(plane_waves, transmission, *tables, probe_pos, probe_pos, wave_index, wave_weight, wave_phase)


def solution(mesh):
    return jax.shard_map(
        functools.partial(shards, mesh.shape["wave"]),
        mesh=mesh,
        in_specs=(
            P(None, "wave", "row", None),
            P(None, None, "row", None),
            P("wave", None),
            P("wave"),
            P("wave"),
            P(),
        ),
        out_specs=P("row", "wave", None),
        check_vma=False,
    )
```

```python
import functools
import math

import jax
import jax.numpy as jnp
import ml_dtypes
import numpy as np
from jax import lax
from jax.experimental import pallas as pl
from jax.experimental.pallas import tpu as pltpu
from jax.sharding import PartitionSpec as P

MESH = pl.DeviceIdType.MESH
F32 = jnp.float32
BF16 = jnp.bfloat16

GRID = 2048
PARTS = 16
LANES = 128
WINDOW = 128
HALF = 64
FACTOR = 16
FRESNEL = 0.1
ROWS_LOAD = 32
BATCH = 2
GROUPS = 11
KEEP = 8 * GROUPS
FIRST = -KEEP // 2
BLOCK = 2 * KEEP
DEPTH = PARTS * BLOCK
CHUNKS = ((0, 5), (5, 9), (9, 11))
PROBES = 8
NT = (((1,), (1,)), ((), ()))


def split_host(table):
    table = np.asarray(table, np.float32)
    high = table.astype(ml_dtypes.bfloat16)
    low = (table - high.astype(np.float32)).astype(ml_dtypes.bfloat16)
    return high, low


def host_tables(wave_count):
    lane = np.arange(LANES)
    freq = np.arange(KEEP) + FIRST
    group, part, member = np.meshgrid(np.arange(GROUPS), np.arange(2), np.arange(8), indexing="ij")
    row_freq = (group * 8 + member).reshape(-1) + FIRST
    row_imag = part.reshape(-1)

    angle = 2 * math.pi * (row_freq[:, None] * lane[None, :] % LANES) / LANES
    imag = row_imag[:, None] == 1
    forward_x = np.concatenate(
        [np.where(imag, -np.sin(angle), np.cos(angle)), np.where(imag, np.cos(angle), np.sin(angle))], axis=1
    )
    high, low = split_host(forward_x)
    forward_x = np.concatenate([high, high, low], axis=1)

    angle = 2 * math.pi * (lane[:, None] * freq[None, :] % LANES) / LANES
    pad = np.zeros((LANES, LANES - KEEP))
    cos = np.concatenate([np.cos(angle), pad], axis=1)
    sin = np.concatenate([np.sin(angle), pad], axis=1)
    forward_y = np.block([[cos, -sin], [sin, cos]])
    inverse_y = np.block([[cos.T, sin.T], [-sin.T, cos.T]])
    high, low = split_host(forward_y)
    forward_y = np.concatenate([high, high, low], axis=0)
    high, low = split_host(inverse_y)
    inverse_y = np.concatenate([high, high, low], axis=0)

    k1 = np.arange(PARTS)
    angle = -2 * math.pi * (k1[:, None] * lane[None, :]) / GRID
    twiddle = np.stack([np.cos(angle), np.sin(angle)], axis=1).astype(np.float32)
    twiddle = np.ascontiguousarray(np.broadcast_to(twiddle[:, :, None, :], (PARTS, 2, 8, LANES)))

    ky = k1[:, None] + 16 * np.concatenate([freq, np.full(LANES - KEEP, 4 * GRID)])[None, :]
    angle = -math.pi * FRESNEL / GRID * (ky.astype(np.float64) ** 2) - 2 * math.pi * (HALF * ky % GRID) / GRID
    inside = np.abs(ky) < GRID
    scale = inside / float(GRID * GRID)
    prop = np.stack([scale * np.cos(angle), scale * np.sin(angle)], axis=1).astype(np.float32)
    nine = np.where(inside, 9 * ky * ky, 2**30).astype(np.int32)[:, None, :]

    depth_kx, depth_imag = [], []
    for begin, end in CHUNKS:
        for source in range(PARTS):
            rows = slice(16 * begin, 16 * end)
            depth_kx.append(source + 16 * row_freq[rows])
            depth_imag.append(row_imag[rows])
    depth_kx = np.concatenate(depth_kx)
    depth_imag = np.concatenate(depth_imag)
    order = np.arange(WINDOW)
    mu = depth_kx[None, :] - 16 * order[:, None]
    dirichlet = np.zeros(mu.shape)
    for m in range(WINDOW // 2):
        dirichlet += 2 * np.cos(math.pi * ((2 * m + 1) * mu % (2 * GRID)) / GRID)
    dirichlet = dirichlet.astype(np.float32)
    fresnel = -math.pi * FRESNEL / GRID * depth_kx.astype(np.float64) ** 2
    fresnel = np.mod(fresnel + math.pi, 2 * math.pi) - math.pi
    phase_f = fresnel.astype(np.float32)[None, :]
    phase_i = np.stack([depth_kx, 1024 * depth_imag]).astype(np.int32)

    share = WINDOW // wave_count
    s, ri, q = np.meshgrid(np.arange(wave_count), np.arange(2), np.arange(share), indexing="ij")
    out_q = (s * share + q).reshape(-1)
    imag = ri.reshape(-1)[:, None] == 1
    angle = 2 * math.pi * (out_q[:, None] * lane[None, :] % LANES) / LANES
    last = np.concatenate(
        [np.where(imag, -np.sin(angle), np.cos(angle)), np.where(imag, np.cos(angle), np.sin(angle))], axis=1
    )
    high, low = split_host(last)
    last = np.concatenate([high, high, low], axis=1)
    return (forward_x, forward_y, inverse_y, twiddle, prop, nine, dirichlet, phase_f, phase_i, last)


def split(x):
    high = x.astype(BF16)
    low = (x - high.astype(F32)).astype(BF16)
    return high, low


def four(values, sign):
    (ar, ai), (br, bi), (cr, ci), (dr, di) = values
    s0r, s0i, s1r, s1i = ar + cr, ai + ci, ar - cr, ai - ci
    s2r, s2i, s3r, s3i = br + dr, bi + di, br - dr, bi - di
    if sign < 0:
        s3r, s3i = s3i, -s3r
        return [(s0r + s2r, s0i + s2i), (s1r + s3r, s1i + s3i), (s0r - s2r, s0i - s2i), (s1r - s3r, s1i - s3i)]
    return [(s0r + s2r, s0i + s2i), (s1r - s3i, s1i + s3r), (s0r - s2r, s0i - s2i), (s1r + s3i, s1i - s3r)]


def turn(value, power, sign):
    re, im = value
    power = power % 16
    if power == 0:
        return value
    if power == 4:
        return (im, -re) if sign < 0 else (-im, re)
    half = math.sqrt(0.5)
    if power == 2:
        if sign < 0:
            return (re + im) * half, (im - re) * half
        return (re - im) * half, (im + re) * half
    if power == 6:
        if sign < 0:
            return (im - re) * half, (re + im) * -half
        return (re + im) * -half, (re - im) * half
    c, s = math.cos(2 * math.pi * power / 16), sign * math.sin(2 * math.pi * power / 16)
    return re * c - im * s, re * s + im * c


def sixteen(values, sign):
    inner = [four([values[4 * a1 + a0] for a1 in range(4)], sign) for a0 in range(4)]
    out = [None] * 16
    for k0 in range(4):
        column = four([turn(inner[a0][k0], a0 * k0, sign) for a0 in range(4)], sign)
        for k1 in range(4):
            out[k0 + 4 * k1] = column[k1]
    return out


def cmul(ar, ai, br, bi):
    return ar * br - ai * bi, ar * bi + ai * br


def body(
    wave_count,
    pw_hbm, tr_hbm, fx_hbm, fy_hbm, iy_hbm, tw_hbm, py_hbm, nine_hbm, dk_hbm, pf_hbm, pi_hbm, last_hbm,
    pos_s, windex, wweight, wphase,
    out_ref,
    pw, tr, fx, fy, iy, tw, py, nine, dk, pf, pi, last,
    yx, send1, recv1, yy, send2, recv2, rows_re, rows_im, a_hi, a_lo, total, send3, recv3,
    load_sem, rows_sem, send1_sem, recv1_sem, send2_sem, recv2_sem, forward_sem, local_sem, send3_sem, recv3_sem,
):
    me = lax.axis_index("row")
    wv = lax.axis_index("wave")
    share = WINDOW // wave_count

    y_lo, z, core = me // 8, lax.rem(me // 2, 4), lax.rem(me, 2)
    chip = me // 2
    sibling = 2 * chip + 1 - core

    def other_chip(n):
        return lax.rem(y_lo + n // 4, 2) * 4 + lax.rem(z + n, 4)

    def other_row(n):
        return 2 * other_chip(lax.rem(n, 8)) + lax.rem(core + n // 8, 2)

    def other_wave(n):
        return lax.rem(wv + n, 4) + lax.rem(wv // 4 + n // 4, 2) * 4

    barrier = pltpu.get_barrier_semaphore()

    def greet_row(d, _):
        pl.semaphore_signal(barrier, inc=1, device_id={"row": other_row(d)}, device_id_type=MESH)
        return 0

    def greet_wave(d, _):
        pl.semaphore_signal(barrier, inc=1, device_id={"wave": other_wave(d)}, device_id_type=MESH)
        return 0

    lax.fori_loop(1, PARTS, greet_row, 0)
    lax.fori_loop(1, wave_count, greet_wave, 0)

    tables = ((fx_hbm, fx), (tw_hbm, tw), (dk_hbm, dk), (pf_hbm, pf), (pi_hbm, pi), (fy_hbm, fy), (iy_hbm, iy),
              (py_hbm, py), (nine_hbm, nine), (last_hbm, last))
    small = [pltpu.make_async_copy(src, dst, load_sem.at[n]) for n, (src, dst) in enumerate(tables)]

    def load_rows(n):
        rows = pl.ds(n * ROWS_LOAD, ROWS_LOAD)
        return (
            pltpu.make_async_copy(pw_hbm.at[:, 0, rows], pw.at[:, rows], rows_sem.at[0, n]),
            pltpu.make_async_copy(tr_hbm.at[0, :, rows], tr.at[:, rows], rows_sem.at[1, n]),
        )

    small[1].start()
    for n in range(LANES // ROWS_LOAD):
        for load in load_rows(n):
            load.start()
    small[0].start()
    for load in small[2:]:
        load.start()
    small[1].wait()

    with jax.named_scope("column_transform"):
        def columns_16(r, _):
            rows = pl.ds(pl.multiple_of(r * 8, 8), 8)
            values = []
            for a in range(PARTS):
                cols = slice(a * LANES, (a + 1) * LANES)
                values.append(cmul(pw[0, rows, cols], pw[1, rows, cols], tr[0, rows, cols], tr[1, rows, cols]))
            for k, (re, im) in enumerate(sixteen(values, -1)):
                if k > 0:
                    re, im = cmul(re, im, tw[k, 0], tw[k, 1])
                yx[k, rows, :LANES] = re
                yx[k, rows, LANES:] = im
            return 0

        for n in range(LANES // ROWS_LOAD):
            for load in load_rows(n):
                load.wait()
            lax.fori_loop(n * ROWS_LOAD // 8, (n + 1) * ROWS_LOAD // 8, columns_16, 0)
        small[0].wait()

    pl.semaphore_wait(barrier, PARTS - 1 + wave_count - 1)

    def copy1(c, peer):
        begin, end = CHUNKS[c]
        rows = pl.ds(16 * begin, 16 * (end - begin))
        return pltpu.make_async_remote_copy(
            src_ref=send1.at[peer, rows], dst_ref=recv1.at[me, rows],
            send_sem=send1_sem.at[c, peer], recv_sem=recv1_sem.at[c, me],
            device_id={"row": peer}, device_id_type=MESH,
        )

    def arrived1(c, source):
        begin, end = CHUNKS[c]
        rows = pl.ds(16 * begin, 16 * (end - begin))
        return pltpu.make_async_remote_copy(
            src_ref=send1.at[source, rows], dst_ref=recv1.at[source, rows],
            send_sem=send1_sem.at[c, source], recv_sem=recv1_sem.at[c, source],
            device_id={"row": source}, device_id_type=MESH,
        )

    with jax.named_scope("column_products"):
        def product(j):
            high, low = split(yx[j])
            return lax.dot_general(
                fx[...], jnp.concatenate([high, low, high], axis=1), NT, preferred_element_type=F32
            )

        def columns_128(d, _):
            j = other_row(d)
            send1[j] = product(j)
            copy1(0, j).start()
            return 0

        lax.fori_loop(1, PARTS, columns_128, 0)
        for c in range(1, len(CHUNKS)):
            def more(d, _):
                copy1(c, other_row(d)).start()
                return 0

            lax.fori_loop(1, PARTS, more, 0)
        recv1[me] = product(me)

    with jax.named_scope("window_weights"):
        for load in small[2:]:
            load.wait()
        probe = lax.broadcasted_iota(jnp.int32, (PROBES, 1), 0)
        r0 = jnp.zeros((PROBES, 1), jnp.int32)
        c0 = jnp.zeros((PROBES, 1), jnp.int32)
        for p in range(PROBES):
            r0 = jnp.where(probe == p, pos_s[0, me * PROBES + p], r0)
            c0 = jnp.where(probe == p, pos_s[1, me * PROBES + p], c0)
        tilt = FACTOR * (r0 * windex[0, 0] + c0 * windex[0, 1])
        units = (2 * (c0 - HALF) + (WINDOW - 1)) * pi[0:1, :] + pi[1:2, :] - 2 * tilt
        units = jnp.bitwise_and(units, 2 * GRID - 1)
        angle = units.astype(F32) * (math.pi / GRID) + pf[...] + wphase[0]
        rows_re[...] = jnp.cos(angle) * wweight[0]
        rows_im[...] = jnp.sin(angle) * wweight[0]

        def weights_of(n, _):
            p, part = n // 8, lax.rem(n, 8)
            rows = pl.ds(pl.multiple_of(part * 16, 16), 16)
            rows2 = pl.ds(pl.multiple_of(part * 16 + WINDOW, 16), 16)
            base = dk[rows, :]
            high, low = split(base * rows_re[pl.ds(p, 1), :])
            a_hi[p, rows, :] = high
            a_lo[p, rows, :] = low
            high, low = split(base * rows_im[pl.ds(p, 1), :])
            a_hi[p, rows2, :] = high
            a_lo[p, rows2, :] = low
            return 0

        lax.fori_loop(0, PROBES * 8, weights_of, 0)

    def slot2(c, source):
        begin, end = CHUNKS[c]
        size = 16 * (end - begin)
        return pl.ds(pl.multiple_of(256 * begin + source * size, 16), size)

    def rows_of(c):
        begin, end = CHUNKS[c]
        return pl.ds(16 * begin, 16 * (end - begin))

    def copy2(c, block, which, target, sem):
        return pltpu.make_async_remote_copy(
            src_ref=send2.at[lax.rem(block, PARTS), rows_of(c)], dst_ref=recv2.at[which, slot2(c, me)],
            send_sem=send2_sem.at[c, sem], recv_sem=recv2_sem.at[c, which, me],
            device_id={"row": target}, device_id_type=MESH,
        )

    def copies2(c, n):
        there = other_chip(n)
        return (
            copy2(c, 2 * there, 0, 2 * there, 3 * n),
            copy2(c, 2 * there + 2, 1, 2 * there + 1, 3 * n + 1),
            copy2(c, 2 * there + 1, 1 - core, 2 * there + core, 3 * n + 2),
        )

    def copy2_sibling(c):
        return copy2(c, 2 * chip + 2 * (1 - core), 1 - core, sibling, 0)

    def forward2(c, n):
        source = 2 * other_chip(n) + core
        return pltpu.make_async_remote_copy(
            src_ref=recv2.at[1 - core, slot2(c, source)], dst_ref=recv2.at[core, slot2(c, source)],
            send_sem=forward_sem.at[c, n], recv_sem=recv2_sem.at[c, core, source],
            device_id={"row": sibling}, device_id_type=MESH,
        )

    def arrived2(c, which, source):
        return pltpu.make_async_remote_copy(
            src_ref=send2.at[source, rows_of(c)], dst_ref=recv2.at[which, slot2(c, source)],
            send_sem=send2_sem.at[c, 0], recv_sem=recv2_sem.at[c, which, source],
            device_id={"row": sibling}, device_id_type=MESH,
        )

    def keep2(c, which, block):
        return pltpu.make_async_copy(
            send2.at[lax.rem(block, PARTS), rows_of(c)], recv2.at[which, slot2(c, me)], local_sem.at[c, which]
        )

    def keeps2(c):
        return keep2(c, core, 2 * chip + 2 * core), keep2(c, 1 - core, 2 * chip + 1)

    for c, (begin, end) in enumerate(CHUNKS):
        size = 8 * (end - begin)
        with jax.named_scope("wait_columns"):
            def wait1(d, _):
                arrived1(c, other_row(d)).wait_recv()
                return 0

            lax.fori_loop(1, PARTS, wait1, 0)

        with jax.named_scope("row_transform"):
            def rows_16(g, _):
                re_rows = pl.ds(pl.multiple_of(g * 16, 8), 8)
                im_rows = pl.ds(pl.multiple_of(g * 16 + 8, 8), 8)
                here = pl.ds(pl.multiple_of((g - begin) * 8, 8), 8)
                values = [(recv1[a, re_rows, :], recv1[a, im_rows, :]) for a in range(PARTS)]
                for k, (re, im) in enumerate(sixteen(values, -1)):
                    if k > 0:
                        re, im = cmul(re, im, tw[k, 0], tw[k, 1])
                    yy[k, here, :LANES] = re
                    yy[k, here, LANES:] = im
                return 0

            lax.fori_loop(begin, end, rows_16, 0)

            kx = me + 16 * (FIRST + 8 * begin + lax.broadcasted_iota(jnp.int32, (1, size, LANES), 1))
            limit = GRID * GRID - 9 * kx * kx

            def products(n, _):
                ks = pl.ds(n * 4, 4)
                y = yy[ks, :size, :].reshape(4 * size, 2 * LANES)
                high, low = split(y)
                f = jnp.dot(jnp.concatenate([high, low, high], axis=1), fy[...], preferred_element_type=F32)
                f = f.reshape(4, size, 2 * LANES)
                re, im = cmul(f[:, :, :LANES], f[:, :, LANES:], py[ks, 0:1, :], py[ks, 1:2, :])
                open_ = nine[ks] <= limit
                re = jnp.where(open_, re, 0.0)
                im = jnp.where(open_, im, 0.0)
                f = jnp.concatenate([re, im], axis=2).reshape(4 * size, 2 * LANES)
                high, low = split(f)
                f = jnp.dot(jnp.concatenate([high, low, high], axis=1), iy[...], preferred_element_type=F32)
                yy[ks, :size, :] = f.reshape(4, size, 2 * LANES)
                return 0

            lax.fori_loop(0, 4, products, 0)

            def rows_back(g, _):
                re_rows = pl.ds(pl.multiple_of(g * 16, 8), 8)
                im_rows = pl.ds(pl.multiple_of(g * 16 + 8, 8), 8)
                here = pl.ds(pl.multiple_of((g - begin) * 8, 8), 8)
                values = []
                for k in range(PARTS):
                    re, im = yy[k, here, :LANES], yy[k, here, LANES:]
                    if k > 0:
                        re, im = cmul(re, im, tw[k, 0], -tw[k, 1])
                    values.append((re, im))
                for a, (re, im) in enumerate(sixteen(values, 1)):
                    send2[a, re_rows, :] = re
                    send2[a, im_rows, :] = im
                return 0

            lax.fori_loop(begin, end, rows_back, 0)

        with jax.named_scope("send_rows"):
            def send(n, _):
                for copy in copies2(c, n):
                    copy.start()
                return 0

            lax.fori_loop(1, PARTS // 2, send, 0)
            copy2_sibling(c).start()
            for copy in keeps2(c):
                copy.start()

    for c, (begin, end) in enumerate(CHUNKS):
        with jax.named_scope("wait_rows"):
            for copy in keeps2(c):
                copy.wait()
            forward2(c, 0).start()

            def shared(n, _):
                arrived2(c, 1 - core, 2 * other_chip(n) + core).wait_recv()
                forward2(c, n).start()
                return 0

            def exclusive(n, _):
                arrived2(c, core, other_row(n)).wait_recv()
                return 0

            def forwarded(n, _):
                arrived2(c, 1 - core, 2 * other_chip(n) + 1 - core).wait_recv()
                return 0

            lax.fori_loop(1, PARTS // 2, shared, 0)
            lax.fori_loop(1, PARTS, exclusive, 0)
            lax.fori_loop(0, PARTS // 2, forwarded, 0)
        with jax.named_scope("window_columns"):
            deep = slice(256 * begin, 256 * end)
            y = jnp.concatenate([recv2[0, deep, :], recv2[1, deep, :]], axis=1)
            high, low = split(y)

            def contract(p):
                t = jnp.dot(a_hi[p, :, deep], high, preferred_element_type=F32)
                t += jnp.dot(a_hi[p, :, deep], low, preferred_element_type=F32)
                t += jnp.dot(a_lo[p, :, deep], high, preferred_element_type=F32)
                return t

            def partial(p, _):
                if c == 0:
                    total[p] = contract(p)
                else:
                    total[p] += contract(p)
                return 0

            if c < len(CHUNKS) - 1:
                lax.fori_loop(0, PROBES, partial, 0)
                continue

            lane = lax.broadcasted_iota(jnp.int32, (1, LANES), 1)

            def copy3(b, peer, slot):
                probes = pl.ds(b * BATCH, BATCH)
                return pltpu.make_async_remote_copy(
                    src_ref=send3.at[peer, probes], dst_ref=recv3.at[slot, probes],
                    send_sem=send3_sem.at[b, peer], recv_sem=recv3_sem.at[b, slot],
                    device_id={"wave": peer}, device_id_type=MESH,
                )

            def finish(p, _):
                offset = pos_s[0, me * PROBES + p] - me * LANES
                t = total[p] + contract(p)
                u = jnp.where(lane >= offset, t[:, :LANES], t[:, LANES:])
                u = jnp.concatenate([u[:WINDOW], u[WINDOW:]], axis=1)
                u_high, u_low = split(u)
                v = lax.dot_general(
                    last[...], jnp.concatenate([u_high, u_low, u_high], axis=1), NT, preferred_element_type=F32
                )
                send3[:, p] = v.reshape(wave_count, 2 * share, LANES)
                return 0

            def batch(b, _):
                lax.fori_loop(b * BATCH, (b + 1) * BATCH, finish, 0)

                def send_sum(n, _):
                    copy3(b, other_wave(n), wv).start()
                    return 0

                lax.fori_loop(1, wave_count, send_sum, 0)
                return 0

            lax.fori_loop(0, PROBES // BATCH, batch, 0)

    with jax.named_scope("add_waves"):
        def collect(b, _):
            def wait3(n, _):
                source = other_wave(n)
                copy3(b, source, source).wait_recv()
                return 0

            lax.fori_loop(1, wave_count, wait3, 0)
            probes = pl.ds(b * BATCH, BATCH)
            v = send3[wv, probes]
            for n in range(1, wave_count):
                v = v + recv3[other_wave(n), probes]
            re, im = v[:, :share], v[:, share:]
            out_ref[probes] = (re * re + im * im) * (1.0 / (WINDOW * WINDOW * wave_count))
            return 0

        lax.fori_loop(0, PROBES // BATCH, collect, 0)

    with jax.named_scope("drain"):
        def drain1(n, _):
            for c in range(len(CHUNKS)):
                copy1(c, other_row(n)).wait_send()
            return 0

        def drain2(n, _):
            for c in range(len(CHUNKS)):
                for copy in copies2(c, n):
                    copy.wait_send()
                forward2(c, n).wait_send()
            return 0

        def drain3(n, _):
            for b in range(PROBES // BATCH):
                copy3(b, other_wave(n), wv).wait_send()
            return 0

        lax.fori_loop(1, PARTS, drain1, 0)
        lax.fori_loop(1, PARTS // 2, drain2, 0)
        for c in range(len(CHUNKS)):
            copy2_sibling(c).wait_send()
            forward2(c, 0).wait_send()
        lax.fori_loop(1, wave_count, drain3, 0)


def shards(wave_count, plane_waves, transmission, wave_index, wave_weight, wave_phase, probe_pos):
    tables = [jnp.asarray(t) for t in host_tables(wave_count)]
    share = WINDOW // wave_count
    rows = plane_waves.shape[2]
    chunks = len(CHUNKS)
    largest = max(8 * (end - begin) for begin, end in CHUNKS)
    any_ = pl.BlockSpec(memory_space=pl.ANY)
    vmem = pl.BlockSpec(memory_space=pltpu.VMEM)
    smem = pl.BlockSpec(memory_space=pltpu.SMEM)
    return pl.pallas_call(
        functools.partial(body, wave_count),
        out_shape=jax.ShapeDtypeStruct((PROBES, share, LANES), F32),
        in_specs=[any_] * 12 + [smem] * 4,
        out_specs=vmem,
        scratch_shapes=[
            pltpu.VMEM((2, rows, GRID), F32),
            pltpu.VMEM((2, rows, GRID), F32),
        ]
        + [pltpu.VMEM(t.shape, t.dtype) for t in tables]
        + [
            pltpu.VMEM((PARTS, LANES, 2 * LANES), F32),
            pltpu.VMEM((PARTS, BLOCK, LANES), F32),
            pltpu.VMEM((PARTS, BLOCK, LANES), F32),
            pltpu.VMEM((PARTS, largest, 2 * LANES), F32),
            pltpu.VMEM((PARTS, BLOCK, LANES), F32),
            pltpu.VMEM((2, DEPTH, LANES), F32),
            pltpu.VMEM((PROBES, DEPTH), F32),
            pltpu.VMEM((PROBES, DEPTH), F32),
            pltpu.VMEM((PROBES, 2 * WINDOW, DEPTH), BF16),
            pltpu.VMEM((PROBES, 2 * WINDOW, DEPTH), BF16),
            pltpu.VMEM((PROBES, 2 * WINDOW, 2 * LANES), F32),
            pltpu.VMEM((wave_count, PROBES, 2 * share, LANES), F32),
            pltpu.VMEM((wave_count, PROBES, 2 * share, LANES), F32),
            pltpu.SemaphoreType.DMA((len(tables),)),
            pltpu.SemaphoreType.DMA((2, LANES // ROWS_LOAD)),
            pltpu.SemaphoreType.DMA((chunks, PARTS)),
            pltpu.SemaphoreType.DMA((chunks, PARTS)),
            pltpu.SemaphoreType.DMA((chunks, 3 * PARTS // 2)),
            pltpu.SemaphoreType.DMA((chunks, 2, PARTS)),
            pltpu.SemaphoreType.DMA((chunks, PARTS // 2)),
            pltpu.SemaphoreType.DMA((chunks, 2)),
            pltpu.SemaphoreType.DMA((PROBES // BATCH, wave_count)),
            pltpu.SemaphoreType.DMA((PROBES // BATCH, wave_count)),
        ],
        compiler_params=pltpu.CompilerParams(
            collective_id=0, has_side_effects=True, vmem_limit_bytes=60 * 1024 * 1024
        ),
    )(plane_waves, transmission, *tables, probe_pos.T, wave_index, wave_weight, wave_phase)


def solution(mesh):
    return jax.shard_map(
        functools.partial(shards, mesh.shape["wave"]),
        mesh=mesh,
        in_specs=(
            P(None, "wave", "row", None),
            P(None, None, "row", None),
            P("wave", None),
            P("wave"),
            P("wave"),
            P(),
        ),
        out_specs=P("row", "wave", None),
        check_vma=False,
    )
```

```python
import functools
import math

import jax
import jax.numpy as jnp
import ml_dtypes
import numpy as np
from jax import lax
from jax.experimental import pallas as pl
from jax.experimental.pallas import tpu as pltpu
from jax.sharding import PartitionSpec as P

MESH = pl.DeviceIdType.MESH
F32 = jnp.float32
BF16 = jnp.bfloat16

GRID = 2048
PARTS = 16
LANES = 128
WINDOW = 128
HALF = 64
FACTOR = 16
FRESNEL = 0.1
ROWS_LOAD = 32
BATCH = 2
GROUPS = 11
KEEP = 8 * GROUPS
FIRST = -KEEP // 2
BLOCK = 2 * KEEP
DEPTH = PARTS * BLOCK
CHUNKS = ((0, 4), (4, 8), (8, 11))
PROBES = 8
WAVE_ORDER = (4, 1, 3, 6, 2, 5, 7)
NT = (((1,), (1,)), ((), ()))


def split_host(table):
    table = np.asarray(table, np.float32)
    high = table.astype(ml_dtypes.bfloat16)
    low = (table - high.astype(np.float32)).astype(ml_dtypes.bfloat16)
    return high, low


def host_tables(wave_count):
    lane = np.arange(LANES)
    freq = np.arange(KEEP) + FIRST
    group, part, member = np.meshgrid(np.arange(GROUPS), np.arange(2), np.arange(8), indexing="ij")
    row_freq = (group * 8 + member).reshape(-1) + FIRST
    row_imag = part.reshape(-1)

    angle = 2 * math.pi * (row_freq[:, None] * lane[None, :] % LANES) / LANES
    imag = row_imag[:, None] == 1
    forward_x = np.concatenate(
        [np.where(imag, -np.sin(angle), np.cos(angle)), np.where(imag, np.cos(angle), np.sin(angle))], axis=1
    )
    high, low = split_host(forward_x)
    forward_x = np.concatenate([high, high, low], axis=1)

    angle = 2 * math.pi * (lane[:, None] * freq[None, :] % LANES) / LANES
    pad = np.zeros((LANES, LANES - KEEP))
    cos = np.concatenate([np.cos(angle), pad], axis=1)
    sin = np.concatenate([np.sin(angle), pad], axis=1)
    forward_y = np.block([[cos, -sin], [sin, cos]])
    inverse_y = np.block([[cos.T, sin.T], [-sin.T, cos.T]])
    high, low = split_host(forward_y)
    forward_y = np.concatenate([high, high, low], axis=0)
    high, low = split_host(inverse_y)
    inverse_y = np.concatenate([high, high, low], axis=0)

    k1 = np.arange(PARTS)
    angle = -2 * math.pi * (k1[:, None] * lane[None, :]) / GRID
    twiddle = np.stack([np.cos(angle), np.sin(angle)], axis=1).astype(np.float32)
    twiddle = np.ascontiguousarray(np.broadcast_to(twiddle[:, :, None, :], (PARTS, 2, 8, LANES)))

    ky = k1[:, None] + 16 * np.concatenate([freq, np.full(LANES - KEEP, 4 * GRID)])[None, :]
    angle = -math.pi * FRESNEL / GRID * (ky.astype(np.float64) ** 2) - 2 * math.pi * (HALF * ky % GRID) / GRID
    inside = np.abs(ky) < GRID
    scale = inside / float(GRID * GRID)
    prop = np.stack([scale * np.cos(angle), scale * np.sin(angle)], axis=1).astype(np.float32)
    nine = np.where(inside, 9 * ky * ky, 2**30).astype(np.int32)[:, None, :]

    depth_kx, depth_imag = [], []
    for begin, end in CHUNKS:
        for source in range(PARTS):
            rows = slice(16 * begin, 16 * end)
            depth_kx.append(source + 16 * row_freq[rows])
            depth_imag.append(row_imag[rows])
    depth_kx = np.concatenate(depth_kx)
    depth_imag = np.concatenate(depth_imag)
    order = np.arange(WINDOW)
    mu = depth_kx[None, :] - 16 * order[:, None]
    dirichlet = np.zeros(mu.shape)
    for m in range(WINDOW // 2):
        dirichlet += 2 * np.cos(math.pi * ((2 * m + 1) * mu % (2 * GRID)) / GRID)
    dirichlet = dirichlet.astype(np.float32)
    fresnel = -math.pi * FRESNEL / GRID * depth_kx.astype(np.float64) ** 2
    fresnel = np.mod(fresnel + math.pi, 2 * math.pi) - math.pi
    phase_f = fresnel.astype(np.float32)[None, :]
    phase_i = np.stack([depth_kx, 1024 * depth_imag]).astype(np.int32)

    share = WINDOW // wave_count
    s, ri, q = np.meshgrid(np.arange(wave_count), np.arange(2), np.arange(share), indexing="ij")
    out_q = (s * share + q).reshape(-1)
    imag = ri.reshape(-1)[:, None] == 1
    angle = 2 * math.pi * (out_q[:, None] * lane[None, :] % LANES) / LANES
    last = np.concatenate(
        [np.where(imag, -np.sin(angle), np.cos(angle)), np.where(imag, np.cos(angle), np.sin(angle))], axis=1
    )
    high, low = split_host(last)
    last = np.concatenate([high, high, low], axis=1)
    return (forward_x, forward_y, inverse_y, twiddle, prop, nine, dirichlet, phase_f, phase_i, last)


def split(x):
    high = x.astype(BF16)
    low = (x - high.astype(F32)).astype(BF16)
    return high, low


def four(values, sign):
    (ar, ai), (br, bi), (cr, ci), (dr, di) = values
    s0r, s0i, s1r, s1i = ar + cr, ai + ci, ar - cr, ai - ci
    s2r, s2i, s3r, s3i = br + dr, bi + di, br - dr, bi - di
    if sign < 0:
        s3r, s3i = s3i, -s3r
        return [(s0r + s2r, s0i + s2i), (s1r + s3r, s1i + s3i), (s0r - s2r, s0i - s2i), (s1r - s3r, s1i - s3i)]
    return [(s0r + s2r, s0i + s2i), (s1r - s3i, s1i + s3r), (s0r - s2r, s0i - s2i), (s1r + s3i, s1i - s3r)]


def turn(value, power, sign):
    re, im = value
    power = power % 16
    if power == 0:
        return value
    if power == 4:
        return (im, -re) if sign < 0 else (-im, re)
    half = math.sqrt(0.5)
    if power == 2:
        if sign < 0:
            return (re + im) * half, (im - re) * half
        return (re - im) * half, (im + re) * half
    if power == 6:
        if sign < 0:
            return (im - re) * half, (re + im) * -half
        return (re + im) * -half, (re - im) * half
    c, s = math.cos(2 * math.pi * power / 16), sign * math.sin(2 * math.pi * power / 16)
    return re * c - im * s, re * s + im * c


def sixteen(values, sign):
    inner = [four([values[4 * a1 + a0] for a1 in range(4)], sign) for a0 in range(4)]
    out = [None] * 16
    for k0 in range(4):
        column = four([turn(inner[a0][k0], a0 * k0, sign) for a0 in range(4)], sign)
        for k1 in range(4):
            out[k0 + 4 * k1] = column[k1]
    return out


def cmul(ar, ai, br, bi):
    return ar * br - ai * bi, ar * bi + ai * br


def body(
    wave_count,
    pw_hbm, tr_hbm, fx_hbm, fy_hbm, iy_hbm, tw_hbm, py_hbm, nine_hbm, dk_hbm, pf_hbm, pi_hbm, last_hbm,
    pos_hbm, windex_hbm, wweight_hbm, wphase_hbm,
    out_ref,
    pos_s, windex, wweight, wphase,
    pw, tr, fx, fy, iy, tw, py, nine, dk, pf, pi, last,
    yx, send1, recv1, yy, send2, recv2, rows_re, rows_im, a_hi, a_lo, total, send3, recv3,
    load_sem, rows_sem, send1_sem, recv1_sem, send2_sem, recv2_sem, forward_sem, local_sem, send3_sem, recv3_sem,
):
    me = lax.axis_index("row")
    wv = lax.axis_index("wave")
    share = WINDOW // wave_count

    y_lo, z, core = me // 8, lax.rem(me // 2, 4), lax.rem(me, 2)
    chip = me // 2
    sibling = 2 * chip + 1 - core

    def other_chip(n):
        return lax.rem(y_lo + n // 4, 2) * 4 + lax.rem(z + n, 4)

    def other_row(n):
        return 2 * other_chip(lax.rem(n, 8)) + lax.rem(core + n // 8, 2)

    def other_wave(n):
        return lax.rem(wv + n, 4) + lax.rem(wv // 4 + n // 4, 2) * 4

    barrier = pltpu.get_barrier_semaphore()

    def greet_row(d, _):
        pl.semaphore_signal(barrier, inc=1, device_id={"row": other_row(d)}, device_id_type=MESH)
        return 0

    def greet_wave(d, _):
        pl.semaphore_signal(barrier, inc=1, device_id={"wave": other_wave(d)}, device_id_type=MESH)
        return 0

    lax.fori_loop(1, PARTS, greet_row, 0)
    lax.fori_loop(1, wave_count, greet_wave, 0)

    tables = ((fx_hbm, fx), (tw_hbm, tw), (dk_hbm, dk), (pf_hbm, pf), (pi_hbm, pi), (fy_hbm, fy), (iy_hbm, iy),
              (py_hbm, py), (nine_hbm, nine), (last_hbm, last),
              (pos_hbm, pos_s), (windex_hbm, windex), (wweight_hbm, wweight), (wphase_hbm, wphase))
    small = [pltpu.make_async_copy(src, dst, load_sem.at[n]) for n, (src, dst) in enumerate(tables)]

    def load_rows(n):
        rows = pl.ds(n * ROWS_LOAD, ROWS_LOAD)
        return (
            pltpu.make_async_copy(pw_hbm.at[:, 0, rows], pw.at[:, rows], rows_sem.at[0, n]),
            pltpu.make_async_copy(tr_hbm.at[0, :, rows], tr.at[:, rows], rows_sem.at[1, n]),
        )

    small[1].start()
    for n in range(LANES // ROWS_LOAD):
        for load in load_rows(n):
            load.start()
    small[0].start()
    for load in small[2:]:
        load.start()
    small[1].wait()

    with jax.named_scope("column_transform"):
        def columns_16(r, _):
            rows = pl.ds(pl.multiple_of(r * 8, 8), 8)
            values = []
            for a in range(PARTS):
                cols = slice(a * LANES, (a + 1) * LANES)
                values.append(cmul(pw[0, rows, cols], pw[1, rows, cols], tr[0, rows, cols], tr[1, rows, cols]))
            for k, (re, im) in enumerate(sixteen(values, -1)):
                if k > 0:
                    re, im = cmul(re, im, tw[k, 0], tw[k, 1])
                yx[k, rows, :LANES] = re
                yx[k, rows, LANES:] = im
            return 0

        for n in range(LANES // ROWS_LOAD):
            for load in load_rows(n):
                load.wait()
            lax.fori_loop(n * ROWS_LOAD // 8, (n + 1) * ROWS_LOAD // 8, columns_16, 0)
        small[0].wait()

    pl.semaphore_wait(barrier, PARTS - 1 + wave_count - 1)

    def copy1(c, peer):
        begin, end = CHUNKS[c]
        rows = pl.ds(16 * begin, 16 * (end - begin))
        return pltpu.make_async_remote_copy(
            src_ref=send1.at[peer, rows], dst_ref=recv1.at[me, rows],
            send_sem=send1_sem.at[c, peer], recv_sem=recv1_sem.at[c, me],
            device_id={"row": peer}, device_id_type=MESH,
        )

    def arrived1(c, source):
        begin, end = CHUNKS[c]
        rows = pl.ds(16 * begin, 16 * (end - begin))
        return pltpu.make_async_remote_copy(
            src_ref=send1.at[source, rows], dst_ref=recv1.at[source, rows],
            send_sem=send1_sem.at[c, source], recv_sem=recv1_sem.at[c, source],
            device_id={"row": source}, device_id_type=MESH,
        )

    with jax.named_scope("column_products"):
        def product(j):
            high, low = split(yx[j])
            return lax.dot_general(
                fx[...], jnp.concatenate([high, low, high], axis=1), NT, preferred_element_type=F32
            )

        def columns_128(d, _):
            j = other_row(d)
            send1[j] = product(j)
            copy1(0, j).start()
            return 0

        lax.fori_loop(1, PARTS, columns_128, 0)
        for c in range(1, len(CHUNKS)):
            def more(d, _):
                copy1(c, other_row(d)).start()
                return 0

            lax.fori_loop(1, PARTS, more, 0)
        recv1[me] = product(me)

    with jax.named_scope("window_weights"):
        for load in small[2:]:
            load.wait()
        probe = lax.broadcasted_iota(jnp.int32, (PROBES, 1), 0)
        r0 = jnp.zeros((PROBES, 1), jnp.int32)
        c0 = jnp.zeros((PROBES, 1), jnp.int32)
        for p in range(PROBES):
            r0 = jnp.where(probe == p, pos_s[0, me * PROBES + p], r0)
            c0 = jnp.where(probe == p, pos_s[1, me * PROBES + p], c0)
        tilt = FACTOR * (r0 * windex[0, 0] + c0 * windex[0, 1])
        units = (2 * (c0 - HALF) + (WINDOW - 1)) * pi[0:1, :] + pi[1:2, :] - 2 * tilt
        units = jnp.bitwise_and(units, 2 * GRID - 1)
        angle = units.astype(F32) * (math.pi / GRID) + pf[...] + wphase[0, 0]
        rows_re[...] = jnp.cos(angle) * wweight[0, 0]
        rows_im[...] = jnp.sin(angle) * wweight[0, 0]

        def weights_of(n, _):
            p, part = n // 8, lax.rem(n, 8)
            rows = pl.ds(pl.multiple_of(part * 16, 16), 16)
            rows2 = pl.ds(pl.multiple_of(part * 16 + WINDOW, 16), 16)
            base = dk[rows, :]
            high, low = split(base * rows_re[pl.ds(p, 1), :])
            a_hi[p, rows, :] = high
            a_lo[p, rows, :] = low
            high, low = split(base * rows_im[pl.ds(p, 1), :])
            a_hi[p, rows2, :] = high
            a_lo[p, rows2, :] = low
            return 0

        lax.fori_loop(0, PROBES * 8, weights_of, 0)

    def slot2(c, source):
        begin, end = CHUNKS[c]
        size = 16 * (end - begin)
        return pl.ds(pl.multiple_of(256 * begin + source * size, 16), size)

    def rows_of(c):
        begin, end = CHUNKS[c]
        return pl.ds(16 * begin, 16 * (end - begin))

    def copy2(c, block, which, target, sem):
        return pltpu.make_async_remote_copy(
            src_ref=send2.at[lax.rem(block, PARTS), rows_of(c)], dst_ref=recv2.at[which, slot2(c, me)],
            send_sem=send2_sem.at[c, sem], recv_sem=recv2_sem.at[c, which, me],
            device_id={"row": target}, device_id_type=MESH,
        )

    def copies2(c, n):
        there = other_chip(n)
        return (
            copy2(c, 2 * there, 0, 2 * there, 3 * n),
            copy2(c, 2 * there + 2, 1, 2 * there + 1, 3 * n + 1),
            copy2(c, 2 * there + 1, 1 - core, 2 * there + core, 3 * n + 2),
        )

    def copy2_sibling(c):
        return copy2(c, 2 * chip + 2 * (1 - core), 1 - core, sibling, 0)

    def forward2(c, n):
        source = 2 * other_chip(n) + core
        return pltpu.make_async_remote_copy(
            src_ref=recv2.at[1 - core, slot2(c, source)], dst_ref=recv2.at[core, slot2(c, source)],
            send_sem=forward_sem.at[c, n], recv_sem=recv2_sem.at[c, core, source],
            device_id={"row": sibling}, device_id_type=MESH,
        )

    def arrived2(c, which, source):
        return pltpu.make_async_remote_copy(
            src_ref=send2.at[source, rows_of(c)], dst_ref=recv2.at[which, slot2(c, source)],
            send_sem=send2_sem.at[c, 0], recv_sem=recv2_sem.at[c, which, source],
            device_id={"row": sibling}, device_id_type=MESH,
        )

    def keep2(c, which, block):
        return pltpu.make_async_copy(
            send2.at[lax.rem(block, PARTS), rows_of(c)], recv2.at[which, slot2(c, me)], local_sem.at[c, which]
        )

    def keeps2(c):
        return keep2(c, core, 2 * chip + 2 * core), keep2(c, 1 - core, 2 * chip + 1)

    for c, (begin, end) in enumerate(CHUNKS):
        size = 8 * (end - begin)
        with jax.named_scope("wait_columns"):
            def wait1(d, _):
                arrived1(c, other_row(d)).wait_recv()
                return 0

            lax.fori_loop(1, PARTS, wait1, 0)

        with jax.named_scope("row_transform"):
            def rows_16(g, _):
                re_rows = pl.ds(pl.multiple_of(g * 16, 8), 8)
                im_rows = pl.ds(pl.multiple_of(g * 16 + 8, 8), 8)
                here = pl.ds(pl.multiple_of((g - begin) * 8, 8), 8)
                values = [(recv1[a, re_rows, :], recv1[a, im_rows, :]) for a in range(PARTS)]
                for k, (re, im) in enumerate(sixteen(values, -1)):
                    if k > 0:
                        re, im = cmul(re, im, tw[k, 0], tw[k, 1])
                    yy[k, here, :LANES] = re
                    yy[k, here, LANES:] = im
                return 0

            lax.fori_loop(begin, end, rows_16, 0)

            kx = me + 16 * (FIRST + 8 * begin + lax.broadcasted_iota(jnp.int32, (1, size, LANES), 1))
            limit = GRID * GRID - 9 * kx * kx

            def products(n, _):
                ks = pl.ds(n * 4, 4)
                y = yy[ks, :size, :].reshape(4 * size, 2 * LANES)
                high, low = split(y)
                f = jnp.dot(jnp.concatenate([high, low, high], axis=1), fy[...], preferred_element_type=F32)
                f = f.reshape(4, size, 2 * LANES)
                re, im = cmul(f[:, :, :LANES], f[:, :, LANES:], py[ks, 0:1, :], py[ks, 1:2, :])
                open_ = nine[ks] <= limit
                re = jnp.where(open_, re, 0.0)
                im = jnp.where(open_, im, 0.0)
                f = jnp.concatenate([re, im], axis=2).reshape(4 * size, 2 * LANES)
                high, low = split(f)
                f = jnp.dot(jnp.concatenate([high, low, high], axis=1), iy[...], preferred_element_type=F32)
                yy[ks, :size, :] = f.reshape(4, size, 2 * LANES)
                return 0

            lax.fori_loop(0, 4, products, 0)

            def rows_back(g, _):
                re_rows = pl.ds(pl.multiple_of(g * 16, 8), 8)
                im_rows = pl.ds(pl.multiple_of(g * 16 + 8, 8), 8)
                here = pl.ds(pl.multiple_of((g - begin) * 8, 8), 8)
                values = []
                for k in range(PARTS):
                    re, im = yy[k, here, :LANES], yy[k, here, LANES:]
                    if k > 0:
                        re, im = cmul(re, im, tw[k, 0], -tw[k, 1])
                    values.append((re, im))
                for a, (re, im) in enumerate(sixteen(values, 1)):
                    send2[a, re_rows, :] = re
                    send2[a, im_rows, :] = im
                return 0

            lax.fori_loop(begin, end, rows_back, 0)

        with jax.named_scope("send_rows"):
            def send(n, _):
                for copy in copies2(c, n):
                    copy.start()
                return 0

            lax.fori_loop(1, PARTS // 2, send, 0)
            copy2_sibling(c).start()
            for copy in keeps2(c):
                copy.start()

    for c, (begin, end) in enumerate(CHUNKS):
        with jax.named_scope("wait_rows"):
            for copy in keeps2(c):
                copy.wait()
            forward2(c, 0).start()

            def shared(n, _):
                arrived2(c, 1 - core, 2 * other_chip(n) + core).wait_recv()
                forward2(c, n).start()
                return 0

            def exclusive(n, _):
                arrived2(c, core, other_row(n)).wait_recv()
                return 0

            def forwarded(n, _):
                arrived2(c, 1 - core, 2 * other_chip(n) + 1 - core).wait_recv()
                return 0

            lax.fori_loop(1, PARTS // 2, shared, 0)
            lax.fori_loop(1, PARTS, exclusive, 0)
            lax.fori_loop(0, PARTS // 2, forwarded, 0)
        with jax.named_scope("window_columns"):
            deep = slice(256 * begin, 256 * end)
            y = jnp.concatenate([recv2[0, deep, :], recv2[1, deep, :]], axis=1)
            high, low = split(y)

            def contract(p):
                t = jnp.dot(a_hi[p, :, deep], high, preferred_element_type=F32)
                t += jnp.dot(a_hi[p, :, deep], low, preferred_element_type=F32)
                t += jnp.dot(a_lo[p, :, deep], high, preferred_element_type=F32)
                return t

            def partial(p, _):
                if c == 0:
                    total[p] = contract(p)
                else:
                    total[p] += contract(p)
                return 0

            if c < len(CHUNKS) - 1:
                lax.fori_loop(0, PROBES, partial, 0)
                continue

            lane = lax.broadcasted_iota(jnp.int32, (1, LANES), 1)

            def copy3(b, peer, slot):
                probes = pl.ds(b * BATCH, BATCH)
                return pltpu.make_async_remote_copy(
                    src_ref=send3.at[peer, probes], dst_ref=recv3.at[slot, probes],
                    send_sem=send3_sem.at[b, peer], recv_sem=recv3_sem.at[b, slot],
                    device_id={"wave": peer}, device_id_type=MESH,
                )

            def finish(p, _):
                offset = pos_s[0, me * PROBES + p] - me * LANES
                t = total[p] + contract(p)
                u = jnp.where(lane >= offset, t[:, :LANES], t[:, LANES:])
                u = jnp.concatenate([u[:WINDOW], u[WINDOW:]], axis=1)
                u_high, u_low = split(u)
                v = lax.dot_general(
                    last[...], jnp.concatenate([u_high, u_low, u_high], axis=1), NT, preferred_element_type=F32
                )
                send3[:, p] = v.reshape(wave_count, 2 * share, LANES)
                return 0

            def batch(b, _):
                lax.fori_loop(b * BATCH, (b + 1) * BATCH, finish, 0)

                for n in WAVE_ORDER:
                    copy3(b, other_wave(n), wv).start()
                return 0

            lax.fori_loop(0, PROBES // BATCH, batch, 0)

    with jax.named_scope("drain"):
        def drain1(n, _):
            for c in range(len(CHUNKS)):
                copy1(c, other_row(n)).wait_send()
            return 0

        def drain2(n, _):
            for c in range(len(CHUNKS)):
                for copy in copies2(c, n):
                    copy.wait_send()
                forward2(c, n).wait_send()
            return 0

        lax.fori_loop(1, PARTS, drain1, 0)
        lax.fori_loop(1, PARTS // 2, drain2, 0)
        for c in range(len(CHUNKS)):
            copy2_sibling(c).wait_send()
            forward2(c, 0).wait_send()

    with jax.named_scope("add_waves"):
        def collect(b, _):
            for n in WAVE_ORDER:
                copy3(b, other_wave(n), wv).wait_send()
            for n in WAVE_ORDER:
                source = other_wave(n)
                copy3(b, source, source).wait_recv()
            probes = pl.ds(b * BATCH, BATCH)
            v = send3[wv, probes]
            for n in range(1, wave_count):
                v = v + recv3[other_wave(n), probes]
            re, im = v[:, :share], v[:, share:]
            out_ref[probes] = (re * re + im * im) * (1.0 / (WINDOW * WINDOW * wave_count))
            return 0

        lax.fori_loop(0, PROBES // BATCH, collect, 0)


def shards(wave_count, plane_waves, transmission, wave_index, wave_weight, wave_phase, probe_pos):
    tables = [jnp.asarray(t) for t in host_tables(wave_count)]
    share = WINDOW // wave_count
    rows = plane_waves.shape[2]
    chunks = len(CHUNKS)
    largest = max(8 * (end - begin) for begin, end in CHUNKS)
    any_ = pl.BlockSpec(memory_space=pl.ANY)
    vmem = pl.BlockSpec(memory_space=pltpu.VMEM)
    return pl.pallas_call(
        functools.partial(body, wave_count),
        out_shape=jax.ShapeDtypeStruct((PROBES, share, LANES), F32),
        in_specs=[any_] * 16,
        out_specs=vmem,
        scratch_shapes=[
            pltpu.SMEM((2, PARTS * PROBES), jnp.int32),
            pltpu.SMEM((1, 2), jnp.int32),
            pltpu.SMEM((1, 1), F32),
            pltpu.SMEM((1, 1), F32),
            pltpu.VMEM((2, rows, GRID), F32),
            pltpu.VMEM((2, rows, GRID), F32),
        ]
        + [pltpu.VMEM(t.shape, t.dtype) for t in tables]
        + [
            pltpu.VMEM((PARTS, LANES, 2 * LANES), F32),
            pltpu.VMEM((PARTS, BLOCK, LANES), F32),
            pltpu.VMEM((PARTS, BLOCK, LANES), F32),
            pltpu.VMEM((PARTS, largest, 2 * LANES), F32),
            pltpu.VMEM((PARTS, BLOCK, LANES), F32),
            pltpu.VMEM((2, DEPTH, LANES), F32),
            pltpu.VMEM((PROBES, DEPTH), F32),
            pltpu.VMEM((PROBES, DEPTH), F32),
            pltpu.VMEM((PROBES, 2 * WINDOW, DEPTH), BF16),
            pltpu.VMEM((PROBES, 2 * WINDOW, DEPTH), BF16),
            pltpu.VMEM((PROBES, 2 * WINDOW, 2 * LANES), F32),
            pltpu.VMEM((wave_count, PROBES, 2 * share, LANES), F32),
            pltpu.VMEM((wave_count, PROBES, 2 * share, LANES), F32),
            pltpu.SemaphoreType.DMA((len(tables) + 4,)),
            pltpu.SemaphoreType.DMA((2, LANES // ROWS_LOAD)),
            pltpu.SemaphoreType.DMA((chunks, PARTS)),
            pltpu.SemaphoreType.DMA((chunks, PARTS)),
            pltpu.SemaphoreType.DMA((chunks, 3 * PARTS // 2)),
            pltpu.SemaphoreType.DMA((chunks, 2, PARTS)),
            pltpu.SemaphoreType.DMA((chunks, PARTS // 2)),
            pltpu.SemaphoreType.DMA((chunks, 2)),
            pltpu.SemaphoreType.DMA((PROBES // BATCH, wave_count)),
            pltpu.SemaphoreType.DMA((PROBES // BATCH, wave_count)),
        ],
        compiler_params=pltpu.CompilerParams(
            collective_id=0, has_side_effects=True, vmem_limit_bytes=60 * 1024 * 1024
        ),
    )(plane_waves, transmission, *tables, probe_pos.T, wave_index, wave_weight.reshape(1, 1), wave_phase.reshape(1, 1))


def solution(mesh):
    return jax.shard_map(
        functools.partial(shards, mesh.shape["wave"]),
        mesh=mesh,
        in_specs=(
            P(None, "wave", "row", None),
            P(None, None, "row", None),
            P("wave", None),
            P("wave"),
            P("wave"),
            P(),
        ),
        out_specs=P("row", "wave", None),
        check_vma=False,
    )
```

```python
import functools
import math

import jax
import jax.numpy as jnp
import ml_dtypes
import numpy as np
from jax import lax
from jax.experimental import pallas as pl
from jax.experimental.pallas import tpu as pltpu
from jax.sharding import PartitionSpec as P

MESH = pl.DeviceIdType.MESH
F32 = jnp.float32
BF16 = jnp.bfloat16

GRID = 2048
PARTS = 16
LANES = 128
WINDOW = 128
HALF = 64
FACTOR = 16
FRESNEL = 0.1
ROWS_LOAD = 32
BATCH = 2
GROUPS = 11
KEEP = 8 * GROUPS
FIRST = -KEEP // 2
BLOCK = 2 * KEEP
DEPTH = PARTS * BLOCK
CHUNKS = ((0, 5), (5, 9), (9, 11))
PROBES = 8
WAVE_ORDER = (4, 1, 3, 6, 2, 5, 7)
NT = (((1,), (1,)), ((), ()))


def split_host(table):
    table = np.asarray(table, np.float32)
    high = table.astype(ml_dtypes.bfloat16)
    low = (table - high.astype(np.float32)).astype(ml_dtypes.bfloat16)
    return high, low


def host_tables(wave_count):
    lane = np.arange(LANES)
    freq = np.arange(KEEP) + FIRST
    group, part, member = np.meshgrid(np.arange(GROUPS), np.arange(2), np.arange(8), indexing="ij")
    row_freq = (group * 8 + member).reshape(-1) + FIRST
    row_imag = part.reshape(-1)

    angle = 2 * math.pi * (row_freq[:, None] * lane[None, :] % LANES) / LANES
    imag = row_imag[:, None] == 1
    forward_x = np.concatenate(
        [np.where(imag, -np.sin(angle), np.cos(angle)), np.where(imag, np.cos(angle), np.sin(angle))], axis=1
    )
    high, low = split_host(forward_x)
    forward_x = np.concatenate([high, high, low], axis=1)

    angle = 2 * math.pi * (lane[:, None] * freq[None, :] % LANES) / LANES
    pad = np.zeros((LANES, LANES - KEEP))
    cos = np.concatenate([np.cos(angle), pad], axis=1)
    sin = np.concatenate([np.sin(angle), pad], axis=1)
    forward_y = np.block([[cos, -sin], [sin, cos]])
    inverse_y = np.block([[cos.T, sin.T], [-sin.T, cos.T]])
    high, low = split_host(forward_y)
    forward_y = np.concatenate([high, high, low], axis=0)
    high, low = split_host(inverse_y)
    inverse_y = np.concatenate([high, high, low], axis=0)

    k1 = np.arange(PARTS)
    angle = -2 * math.pi * (k1[:, None] * lane[None, :]) / GRID
    twiddle = np.stack([np.cos(angle), np.sin(angle)], axis=1).astype(np.float32)
    twiddle = np.ascontiguousarray(np.broadcast_to(twiddle[:, :, None, :], (PARTS, 2, 8, LANES)))

    ky = k1[:, None] + 16 * np.concatenate([freq, np.full(LANES - KEEP, 4 * GRID)])[None, :]
    angle = -math.pi * FRESNEL / GRID * (ky.astype(np.float64) ** 2) - 2 * math.pi * (HALF * ky % GRID) / GRID
    inside = np.abs(ky) < GRID
    scale = inside / float(GRID * GRID)
    prop = np.stack([scale * np.cos(angle), scale * np.sin(angle)], axis=1).astype(np.float32)
    nine = np.where(inside, 9 * ky * ky, 2**30).astype(np.int32)[:, None, :]

    depth_kx = []
    for begin, end in CHUNKS:
        for source in range(PARTS):
            depth_kx.append(source + 16 * freq[8 * begin:8 * end])
    depth_kx = np.concatenate(depth_kx)
    order = np.arange(WINDOW)
    mu = depth_kx[None, :] - 16 * order[:, None]
    dirichlet = np.zeros(mu.shape)
    for m in range(WINDOW // 2):
        dirichlet += 2 * np.cos(math.pi * ((2 * m + 1) * mu % (2 * GRID)) / GRID)
    dirichlet = dirichlet.astype(np.float32)
    fresnel = -math.pi * FRESNEL / GRID * depth_kx.astype(np.float64) ** 2
    fresnel = np.mod(fresnel + math.pi, 2 * math.pi) - math.pi
    phase_f = fresnel.astype(np.float32)[None, :]
    phase_i = depth_kx.astype(np.int32)[None, :]

    share = WINDOW // wave_count
    s, ri, q = np.meshgrid(np.arange(wave_count), np.arange(2), np.arange(share), indexing="ij")
    out_q = (s * share + q).reshape(-1)
    imag = ri.reshape(-1)[:, None] == 1
    angle = 2 * math.pi * (out_q[:, None] * lane[None, :] % LANES) / LANES
    last = np.concatenate(
        [np.where(imag, -np.sin(angle), np.cos(angle)), np.where(imag, np.cos(angle), np.sin(angle))], axis=1
    )
    high, low = split_host(last)
    last = np.concatenate([high, high, low], axis=1)
    return (forward_x, forward_y, inverse_y, twiddle, prop, nine, dirichlet, phase_f, phase_i, last)


def split(x):
    high = x.astype(BF16)
    low = (x - high.astype(F32)).astype(BF16)
    return high, low


def four(values, sign):
    (ar, ai), (br, bi), (cr, ci), (dr, di) = values
    s0r, s0i, s1r, s1i = ar + cr, ai + ci, ar - cr, ai - ci
    s2r, s2i, s3r, s3i = br + dr, bi + di, br - dr, bi - di
    if sign < 0:
        s3r, s3i = s3i, -s3r
        return [(s0r + s2r, s0i + s2i), (s1r + s3r, s1i + s3i), (s0r - s2r, s0i - s2i), (s1r - s3r, s1i - s3i)]
    return [(s0r + s2r, s0i + s2i), (s1r - s3i, s1i + s3r), (s0r - s2r, s0i - s2i), (s1r + s3i, s1i - s3r)]


def turn(value, power, sign):
    re, im = value
    power = power % 16
    if power == 0:
        return value
    if power == 4:
        return (im, -re) if sign < 0 else (-im, re)
    half = math.sqrt(0.5)
    if power == 2:
        if sign < 0:
            return (re + im) * half, (im - re) * half
        return (re - im) * half, (im + re) * half
    if power == 6:
        if sign < 0:
            return (im - re) * half, (re + im) * -half
        return (re + im) * -half, (re - im) * half
    c, s = math.cos(2 * math.pi * power / 16), sign * math.sin(2 * math.pi * power / 16)
    return re * c - im * s, re * s + im * c


def sixteen(values, sign):
    inner = [four([values[4 * a1 + a0] for a1 in range(4)], sign) for a0 in range(4)]
    out = [None] * 16
    for k0 in range(4):
        column = four([turn(inner[a0][k0], a0 * k0, sign) for a0 in range(4)], sign)
        for k1 in range(4):
            out[k0 + 4 * k1] = column[k1]
    return out


def cmul(ar, ai, br, bi):
    return ar * br - ai * bi, ar * bi + ai * br


def body(
    wave_count,
    pw_hbm, tr_hbm, fx_hbm, fy_hbm, iy_hbm, tw_hbm, py_hbm, nine_hbm, dk_hbm, pf_hbm, pi_hbm, last_hbm,
    pos_hbm, windex_hbm, wweight_hbm, wphase_hbm,
    out_ref,
    pos_s, windex, wweight, wphase,
    pw, tr, fx, fy, iy, tw, py, nine, dk, pf, pi, last,
    yx, send1, recv1, yy, send2, recv2, rows_re, rows_im, a_hi, a_lo, total, send3, recv3,
    load_sem, rows_sem, send1_sem, recv1_sem, send2_sem, recv2_sem, forward_sem, local_sem, send3_sem, recv3_sem,
):
    me = lax.axis_index("row")
    wv = lax.axis_index("wave")
    share = WINDOW // wave_count

    y_lo, z, core = me // 8, lax.rem(me // 2, 4), lax.rem(me, 2)
    chip = me // 2
    sibling = 2 * chip + 1 - core

    def other_chip(n):
        return lax.rem(y_lo + n // 4, 2) * 4 + lax.rem(z + n, 4)

    def other_row(n):
        return 2 * other_chip(lax.rem(n, 8)) + lax.rem(core + n // 8, 2)

    def other_wave(n):
        return lax.rem(wv + n, 4) + lax.rem(wv // 4 + n // 4, 2) * 4

    barrier = pltpu.get_barrier_semaphore()

    def greet_row(d, _):
        pl.semaphore_signal(barrier, inc=1, device_id={"row": other_row(d)}, device_id_type=MESH)
        return 0

    def greet_wave(d, _):
        pl.semaphore_signal(barrier, inc=1, device_id={"wave": other_wave(d)}, device_id_type=MESH)
        return 0

    lax.fori_loop(1, PARTS, greet_row, 0)
    lax.fori_loop(1, wave_count, greet_wave, 0)

    tables = ((fx_hbm, fx), (tw_hbm, tw), (dk_hbm, dk), (pf_hbm, pf), (pi_hbm, pi), (fy_hbm, fy), (iy_hbm, iy),
              (py_hbm, py), (nine_hbm, nine), (last_hbm, last),
              (pos_hbm, pos_s), (windex_hbm, windex), (wweight_hbm, wweight), (wphase_hbm, wphase))
    small = [pltpu.make_async_copy(src, dst, load_sem.at[n]) for n, (src, dst) in enumerate(tables)]

    def load_rows(n):
        rows = pl.ds(n * ROWS_LOAD, ROWS_LOAD)
        return (
            pltpu.make_async_copy(pw_hbm.at[:, 0, rows], pw.at[:, rows], rows_sem.at[0, n]),
            pltpu.make_async_copy(tr_hbm.at[0, :, rows], tr.at[:, rows], rows_sem.at[1, n]),
        )

    small[1].start()
    for n in range(LANES // ROWS_LOAD):
        for load in load_rows(n):
            load.start()
    small[0].start()
    for load in small[2:]:
        load.start()
    small[1].wait()

    with jax.named_scope("column_transform"):
        def columns_16(r, _):
            rows = pl.ds(pl.multiple_of(r * 8, 8), 8)
            values = []
            for a in range(PARTS):
                cols = slice(a * LANES, (a + 1) * LANES)
                values.append(cmul(pw[0, rows, cols], pw[1, rows, cols], tr[0, rows, cols], tr[1, rows, cols]))
            for k, (re, im) in enumerate(sixteen(values, -1)):
                if k > 0:
                    re, im = cmul(re, im, tw[k, 0], tw[k, 1])
                yx[k, rows, :LANES] = re
                yx[k, rows, LANES:] = im
            return 0

        for n in range(LANES // ROWS_LOAD):
            for load in load_rows(n):
                load.wait()
            lax.fori_loop(n * ROWS_LOAD // 8, (n + 1) * ROWS_LOAD // 8, columns_16, 0)
        small[0].wait()

    pl.semaphore_wait(barrier, PARTS - 1 + wave_count - 1)

    def copy1(c, peer):
        begin, end = CHUNKS[c]
        rows = pl.ds(16 * begin, 16 * (end - begin))
        return pltpu.make_async_remote_copy(
            src_ref=send1.at[peer, rows], dst_ref=recv1.at[me, rows],
            send_sem=send1_sem.at[c, peer], recv_sem=recv1_sem.at[c, me],
            device_id={"row": peer}, device_id_type=MESH,
        )

    def arrived1(c, source):
        begin, end = CHUNKS[c]
        rows = pl.ds(16 * begin, 16 * (end - begin))
        return pltpu.make_async_remote_copy(
            src_ref=send1.at[source, rows], dst_ref=recv1.at[source, rows],
            send_sem=send1_sem.at[c, source], recv_sem=recv1_sem.at[c, source],
            device_id={"row": source}, device_id_type=MESH,
        )

    with jax.named_scope("column_products"):
        def product(j):
            high, low = split(yx[j])
            return lax.dot_general(
                fx[...], jnp.concatenate([high, low, high], axis=1), NT, preferred_element_type=F32
            )

        def columns_128(d, _):
            j = other_row(d)
            send1[j] = product(j)
            copy1(0, j).start()
            return 0

        lax.fori_loop(1, PARTS, columns_128, 0)
        for c in range(1, len(CHUNKS)):
            def more(d, _):
                copy1(c, other_row(d)).start()
                return 0

            lax.fori_loop(1, PARTS, more, 0)
        recv1[me] = product(me)

    with jax.named_scope("window_weights"):
        for load in small[2:]:
            load.wait()
        probe = lax.broadcasted_iota(jnp.int32, (PROBES, 1), 0)
        r0 = jnp.zeros((PROBES, 1), jnp.int32)
        c0 = jnp.zeros((PROBES, 1), jnp.int32)
        for p in range(PROBES):
            r0 = jnp.where(probe == p, pos_s[0, me * PROBES + p], r0)
            c0 = jnp.where(probe == p, pos_s[1, me * PROBES + p], c0)
        tilt = FACTOR * (r0 * windex[0, 0] + c0 * windex[0, 1])
        units = (2 * (c0 - HALF) + (WINDOW - 1)) * pi[...] - 2 * tilt
        units = jnp.bitwise_and(units, 2 * GRID - 1)
        angle = units.astype(F32) * (math.pi / GRID) + pf[...] + wphase[0, 0]
        rows_re[...] = jnp.cos(angle) * wweight[0, 0]
        rows_im[...] = jnp.sin(angle) * wweight[0, 0]

        def weights_of(n, _):
            p, part = n // 8, lax.rem(n, 8)
            base = dk[pl.ds(pl.multiple_of(part * 16, 16), 16), :]
            rows = pl.ds(pl.multiple_of(n * 16, 16), 16)
            re, im = rows_re[pl.ds(p, 1), :], rows_im[pl.ds(p, 1), :]
            for kind, factor in enumerate((re, re + im, im - re)):
                high, low = split(base * factor)
                a_hi[kind, rows, :] = high
                a_lo[kind, rows, :] = low
            return 0

        lax.fori_loop(0, PROBES * 8, weights_of, 0)

    def slot2(c, source):
        begin, end = CHUNKS[c]
        size = 16 * (end - begin)
        return pl.ds(pl.multiple_of(256 * begin + source * size, 16), size)

    def rows_of(c):
        begin, end = CHUNKS[c]
        return pl.ds(16 * begin, 16 * (end - begin))

    def copy2(c, block, which, target, sem):
        return pltpu.make_async_remote_copy(
            src_ref=send2.at[lax.rem(block, PARTS), rows_of(c)], dst_ref=recv2.at[which, slot2(c, me)],
            send_sem=send2_sem.at[c, sem], recv_sem=recv2_sem.at[c, which, me],
            device_id={"row": target}, device_id_type=MESH,
        )

    def copies2(c, n):
        there = other_chip(n)
        return (
            copy2(c, 2 * there, 0, 2 * there, 3 * n),
            copy2(c, 2 * there + 2, 1, 2 * there + 1, 3 * n + 1),
            copy2(c, 2 * there + 1, 1 - core, 2 * there + core, 3 * n + 2),
        )

    def copy2_sibling(c):
        return copy2(c, 2 * chip + 2 * (1 - core), 1 - core, sibling, 0)

    def forward2(c, n):
        source = 2 * other_chip(n) + core
        return pltpu.make_async_remote_copy(
            src_ref=recv2.at[1 - core, slot2(c, source)], dst_ref=recv2.at[core, slot2(c, source)],
            send_sem=forward_sem.at[c, n], recv_sem=recv2_sem.at[c, core, source],
            device_id={"row": sibling}, device_id_type=MESH,
        )

    def arrived2(c, which, source):
        return pltpu.make_async_remote_copy(
            src_ref=send2.at[source, rows_of(c)], dst_ref=recv2.at[which, slot2(c, source)],
            send_sem=send2_sem.at[c, 0], recv_sem=recv2_sem.at[c, which, source],
            device_id={"row": sibling}, device_id_type=MESH,
        )

    def keep2(c, which, block):
        return pltpu.make_async_copy(
            send2.at[lax.rem(block, PARTS), rows_of(c)], recv2.at[which, slot2(c, me)], local_sem.at[c, which]
        )

    def keeps2(c):
        return keep2(c, core, 2 * chip + 2 * core), keep2(c, 1 - core, 2 * chip + 1)

    for c, (begin, end) in enumerate(CHUNKS):
        size = 8 * (end - begin)
        with jax.named_scope("wait_columns"):
            def wait1(d, _):
                arrived1(c, other_row(d)).wait_recv()
                return 0

            lax.fori_loop(1, PARTS, wait1, 0)

        with jax.named_scope("row_transform"):
            def rows_16(g, _):
                re_rows = pl.ds(pl.multiple_of(g * 16, 8), 8)
                im_rows = pl.ds(pl.multiple_of(g * 16 + 8, 8), 8)
                here = pl.ds(pl.multiple_of((g - begin) * 8, 8), 8)
                values = [(recv1[a, re_rows, :], recv1[a, im_rows, :]) for a in range(PARTS)]
                for k, (re, im) in enumerate(sixteen(values, -1)):
                    if k > 0:
                        re, im = cmul(re, im, tw[k, 0], tw[k, 1])
                    yy[k, here, :LANES] = re
                    yy[k, here, LANES:] = im
                return 0

            lax.fori_loop(begin, end, rows_16, 0)

            kx = me + 16 * (FIRST + 8 * begin + lax.broadcasted_iota(jnp.int32, (1, size, LANES), 1))
            limit = GRID * GRID - 9 * kx * kx

            def products(n, _):
                ks = pl.ds(n * 4, 4)
                y = yy[ks, :size, :].reshape(4 * size, 2 * LANES)
                high, low = split(y)
                f = jnp.dot(jnp.concatenate([high, low, high], axis=1), fy[...], preferred_element_type=F32)
                f = f.reshape(4, size, 2 * LANES)
                re, im = cmul(f[:, :, :LANES], f[:, :, LANES:], py[ks, 0:1, :], py[ks, 1:2, :])
                open_ = nine[ks] <= limit
                re = jnp.where(open_, re, 0.0)
                im = jnp.where(open_, im, 0.0)
                f = jnp.concatenate([re, im], axis=2).reshape(4 * size, 2 * LANES)
                high, low = split(f)
                f = jnp.dot(jnp.concatenate([high, low, high], axis=1), iy[...], preferred_element_type=F32)
                yy[ks, :size, :] = f.reshape(4, size, 2 * LANES)
                return 0

            lax.fori_loop(0, 4, products, 0)

            def rows_back(g, _):
                re_rows = pl.ds(pl.multiple_of(g * 16, 8), 8)
                im_rows = pl.ds(pl.multiple_of(g * 16 + 8, 8), 8)
                here = pl.ds(pl.multiple_of((g - begin) * 8, 8), 8)
                values = []
                for k in range(PARTS):
                    re, im = yy[k, here, :LANES], yy[k, here, LANES:]
                    if k > 0:
                        re, im = cmul(re, im, tw[k, 0], -tw[k, 1])
                    values.append((re, im))
                for a, (re, im) in enumerate(sixteen(values, 1)):
                    send2[a, re_rows, :] = re
                    send2[a, im_rows, :] = im
                return 0

            lax.fori_loop(begin, end, rows_back, 0)

        with jax.named_scope("send_rows"):
            def send(n, _):
                for copy in copies2(c, n):
                    copy.start()
                return 0

            lax.fori_loop(1, PARTS // 2, send, 0)
            copy2_sibling(c).start()
            for copy in keeps2(c):
                copy.start()

    for c, (begin, end) in enumerate(CHUNKS):
        with jax.named_scope("wait_rows"):
            for copy in keeps2(c):
                copy.wait()
            forward2(c, 0).start()

            def shared(n, _):
                arrived2(c, 1 - core, 2 * other_chip(n) + core).wait_recv()
                forward2(c, n).start()
                return 0

            def exclusive(n, _):
                arrived2(c, core, other_row(n)).wait_recv()
                return 0

            def forwarded(n, _):
                arrived2(c, 1 - core, 2 * other_chip(n) + 1 - core).wait_recv()
                return 0

            lax.fori_loop(1, PARTS // 2, shared, 0)
            lax.fori_loop(1, PARTS, exclusive, 0)
            lax.fori_loop(0, PARTS // 2, forwarded, 0)
        with jax.named_scope("window_columns"):
            deep = slice(128 * begin, 128 * end)
            y = jnp.concatenate(
                [recv2[0, 256 * begin:256 * end, :], recv2[1, 256 * begin:256 * end, :]], axis=1
            ).reshape(16 * (end - begin), 2, 8, 2 * LANES)
            size = 128 * (end - begin)
            y_re, y_im = y[:, 0].reshape(size, 2 * LANES), y[:, 1].reshape(size, 2 * LANES)
            stacks = []
            for part in (y_re + y_im, y_im, y_re):
                high, low = split(part)
                stacks.append(jnp.concatenate([high, low, high], axis=0))

            def contract(b):
                rows = pl.ds(pl.multiple_of(b * BATCH * WINDOW, 16), BATCH * WINDOW)
                sums = []
                for kind in range(3):
                    high = a_hi[kind, rows, deep]
                    both = jnp.concatenate([high, high, a_lo[kind, rows, deep]], axis=1)
                    sums.append(jnp.dot(both, stacks[kind], preferred_element_type=F32))
                re, im = sums[0] - sums[1], sums[0] + sums[2]
                if c > 0:
                    re, im = re + total[0, rows, :], im + total[1, rows, :]
                return rows, re, im

            def partial(b, _):
                rows, re, im = contract(b)
                total[0, rows, :] = re
                total[1, rows, :] = im
                return 0

            if c < len(CHUNKS) - 1:
                lax.fori_loop(0, PROBES // BATCH, partial, 0)
                continue

            lane = lax.broadcasted_iota(jnp.int32, (1, LANES), 1)

            def copy3(b, peer, slot):
                probes = pl.ds(b * BATCH, BATCH)
                return pltpu.make_async_remote_copy(
                    src_ref=send3.at[peer, probes], dst_ref=recv3.at[slot, probes],
                    send_sem=send3_sem.at[b, peer], recv_sem=recv3_sem.at[b, slot],
                    device_id={"wave": peer}, device_id_type=MESH,
                )

            def batch(b, _):
                _, re, im = contract(b)
                for n in range(BATCH):
                    p = b * BATCH + n
                    offset = pos_s[0, me * PROBES + p] - me * LANES
                    here = slice(n * WINDOW, (n + 1) * WINDOW)
                    u = jnp.concatenate(
                        [jnp.where(lane >= offset, t[here, :LANES], t[here, LANES:]) for t in (re, im)], axis=1
                    )
                    u_high, u_low = split(u)
                    v = lax.dot_general(
                        last[...], jnp.concatenate([u_high, u_low, u_high], axis=1), NT, preferred_element_type=F32
                    )
                    send3[:, p] = v.reshape(wave_count, 2 * share, LANES)

                for n in WAVE_ORDER:
                    copy3(b, other_wave(n), wv).start()
                return 0

            lax.fori_loop(0, PROBES // BATCH, batch, 0)

    with jax.named_scope("drain"):
        def drain1(n, _):
            for c in range(len(CHUNKS)):
                copy1(c, other_row(n)).wait_send()
            return 0

        def drain2(n, _):
            for c in range(len(CHUNKS)):
                for copy in copies2(c, n):
                    copy.wait_send()
                forward2(c, n).wait_send()
            return 0

        lax.fori_loop(1, PARTS, drain1, 0)
        lax.fori_loop(1, PARTS // 2, drain2, 0)
        for c in range(len(CHUNKS)):
            copy2_sibling(c).wait_send()
            forward2(c, 0).wait_send()

    with jax.named_scope("add_waves"):
        def collect(b, _):
            for n in WAVE_ORDER:
                copy3(b, other_wave(n), wv).wait_send()
            for n in WAVE_ORDER:
                source = other_wave(n)
                copy3(b, source, source).wait_recv()
            probes = pl.ds(b * BATCH, BATCH)
            v = send3[wv, probes]
            for n in range(1, wave_count):
                v = v + recv3[other_wave(n), probes]
            re, im = v[:, :share], v[:, share:]
            out_ref[probes] = (re * re + im * im) * (1.0 / (WINDOW * WINDOW * wave_count))
            return 0

        lax.fori_loop(0, PROBES // BATCH, collect, 0)


def shards(wave_count, plane_waves, transmission, wave_index, wave_weight, wave_phase, probe_pos):
    tables = [jnp.asarray(t) for t in host_tables(wave_count)]
    share = WINDOW // wave_count
    rows = plane_waves.shape[2]
    chunks = len(CHUNKS)
    largest = max(8 * (end - begin) for begin, end in CHUNKS)
    any_ = pl.BlockSpec(memory_space=pl.ANY)
    vmem = pl.BlockSpec(memory_space=pltpu.VMEM)
    return pl.pallas_call(
        functools.partial(body, wave_count),
        out_shape=jax.ShapeDtypeStruct((PROBES, share, LANES), F32),
        in_specs=[any_] * 16,
        out_specs=vmem,
        scratch_shapes=[
            pltpu.SMEM((2, PARTS * PROBES), jnp.int32),
            pltpu.SMEM((1, 2), jnp.int32),
            pltpu.SMEM((1, 1), F32),
            pltpu.SMEM((1, 1), F32),
            pltpu.VMEM((2, rows, GRID), F32),
            pltpu.VMEM((2, rows, GRID), F32),
        ]
        + [pltpu.VMEM(t.shape, t.dtype) for t in tables]
        + [
            pltpu.VMEM((PARTS, LANES, 2 * LANES), F32),
            pltpu.VMEM((PARTS, BLOCK, LANES), F32),
            pltpu.VMEM((PARTS, BLOCK, LANES), F32),
            pltpu.VMEM((PARTS, largest, 2 * LANES), F32),
            pltpu.VMEM((PARTS, BLOCK, LANES), F32),
            pltpu.VMEM((2, DEPTH, LANES), F32),
            pltpu.VMEM((PROBES, DEPTH // 2), F32),
            pltpu.VMEM((PROBES, DEPTH // 2), F32),
            pltpu.VMEM((3, PROBES * WINDOW, DEPTH // 2), BF16),
            pltpu.VMEM((3, PROBES * WINDOW, DEPTH // 2), BF16),
            pltpu.VMEM((2, PROBES * WINDOW, 2 * LANES), F32),
            pltpu.VMEM((wave_count, PROBES, 2 * share, LANES), F32),
            pltpu.VMEM((wave_count, PROBES, 2 * share, LANES), F32),
            pltpu.SemaphoreType.DMA((len(tables) + 4,)),
            pltpu.SemaphoreType.DMA((2, LANES // ROWS_LOAD)),
            pltpu.SemaphoreType.DMA((chunks, PARTS)),
            pltpu.SemaphoreType.DMA((chunks, PARTS)),
            pltpu.SemaphoreType.DMA((chunks, 3 * PARTS // 2)),
            pltpu.SemaphoreType.DMA((chunks, 2, PARTS)),
            pltpu.SemaphoreType.DMA((chunks, PARTS // 2)),
            pltpu.SemaphoreType.DMA((chunks, 2)),
            pltpu.SemaphoreType.DMA((PROBES // BATCH, wave_count)),
            pltpu.SemaphoreType.DMA((PROBES // BATCH, wave_count)),
        ],
        compiler_params=pltpu.CompilerParams(
            collective_id=0, has_side_effects=True, vmem_limit_bytes=60 * 1024 * 1024
        ),
    )(plane_waves, transmission, *tables, probe_pos.T, wave_index, wave_weight.reshape(1, 1), wave_phase.reshape(1, 1))


def solution(mesh):
    return jax.shard_map(
        functools.partial(shards, mesh.shape["wave"]),
        mesh=mesh,
        in_specs=(
            P(None, "wave", "row", None),
            P(None, None, "row", None),
            P("wave", None),
            P("wave"),
            P("wave"),
            P(),
        ),
        out_specs=P("row", "wave", None),
        check_vma=False,
    )
```

```python
import functools
import math

import jax
import jax.numpy as jnp
import ml_dtypes
import numpy as np
from jax import lax
from jax.experimental import pallas as pl
from jax.experimental.pallas import tpu as pltpu
from jax.sharding import PartitionSpec as P

MESH = pl.DeviceIdType.MESH
F32 = jnp.float32
BF16 = jnp.bfloat16

GRID = 2048
PARTS = 16
LANES = 128
WINDOW = 128
HALF = 64
FACTOR = 16
FRESNEL = 0.1
ROWS_LOAD = 32
BATCH = 2
GROUPS = 11
KEEP = 8 * GROUPS
FIRST = -KEEP // 2
BLOCK = 2 * KEEP
DEPTH = PARTS * BLOCK
CHUNKS = ((0, 5), (5, 9), (9, 11))
PROBES = 8
WAVE_ORDER = (4, 1, 3, 6, 2, 5, 7)
ROUTED = (2, 2)
NT = (((1,), (1,)), ((), ()))


def split_host(table):
    table = np.asarray(table, np.float32)
    high = table.astype(ml_dtypes.bfloat16)
    low = (table - high.astype(np.float32)).astype(ml_dtypes.bfloat16)
    return high, low


def host_tables(wave_count):
    lane = np.arange(LANES)
    freq = np.arange(KEEP) + FIRST
    group, part, member = np.meshgrid(np.arange(GROUPS), np.arange(2), np.arange(8), indexing="ij")
    row_freq = (group * 8 + member).reshape(-1) + FIRST
    row_imag = part.reshape(-1)

    angle = 2 * math.pi * (row_freq[:, None] * lane[None, :] % LANES) / LANES
    imag = row_imag[:, None] == 1
    forward_x = np.concatenate(
        [np.where(imag, -np.sin(angle), np.cos(angle)), np.where(imag, np.cos(angle), np.sin(angle))], axis=1
    )
    high, low = split_host(forward_x)
    forward_x = np.concatenate([high, high, low], axis=1)

    angle = 2 * math.pi * (lane[:, None] * freq[None, :] % LANES) / LANES
    pad = np.zeros((LANES, LANES - KEEP))
    cos = np.concatenate([np.cos(angle), pad], axis=1)
    sin = np.concatenate([np.sin(angle), pad], axis=1)
    forward_y = np.block([[cos, -sin], [sin, cos]])
    inverse_y = np.block([[cos.T, sin.T], [-sin.T, cos.T]])
    high, low = split_host(forward_y)
    forward_y = np.concatenate([high, high, low], axis=0)
    high, low = split_host(inverse_y)
    inverse_y = np.concatenate([high, high, low], axis=0)

    k1 = np.arange(PARTS)
    angle = -2 * math.pi * (k1[:, None] * lane[None, :]) / GRID
    twiddle = np.stack([np.cos(angle), np.sin(angle)], axis=1).astype(np.float32)
    twiddle = np.ascontiguousarray(np.broadcast_to(twiddle[:, :, None, :], (PARTS, 2, 8, LANES)))

    ky = k1[:, None] + 16 * np.concatenate([freq, np.full(LANES - KEEP, 4 * GRID)])[None, :]
    angle = -math.pi * FRESNEL / GRID * (ky.astype(np.float64) ** 2) - 2 * math.pi * (HALF * ky % GRID) / GRID
    inside = np.abs(ky) < GRID
    scale = inside / float(GRID * GRID)
    prop = np.stack([scale * np.cos(angle), scale * np.sin(angle)], axis=1).astype(np.float32)
    nine = np.where(inside, 9 * ky * ky, 2**30).astype(np.int32)[:, None, :]

    depth_kx = []
    for begin, end in CHUNKS:
        for source in range(PARTS):
            depth_kx.append(source + 16 * freq[8 * begin:8 * end])
    depth_kx = np.concatenate(depth_kx)
    order = np.arange(WINDOW)
    mu = depth_kx[None, :] - 16 * order[:, None]
    dirichlet = np.zeros(mu.shape)
    for m in range(WINDOW // 2):
        dirichlet += 2 * np.cos(math.pi * ((2 * m + 1) * mu % (2 * GRID)) / GRID)
    dirichlet = dirichlet.astype(np.float32)
    fresnel = -math.pi * FRESNEL / GRID * depth_kx.astype(np.float64) ** 2
    fresnel = np.mod(fresnel + math.pi, 2 * math.pi) - math.pi
    phase_f = fresnel.astype(np.float32)[None, :]
    phase_i = depth_kx.astype(np.int32)[None, :]

    share = WINDOW // wave_count
    s, ri, q = np.meshgrid(np.arange(wave_count), np.arange(2), np.arange(share), indexing="ij")
    out_q = (s * share + q).reshape(-1)
    imag = ri.reshape(-1)[:, None] == 1
    angle = 2 * math.pi * (out_q[:, None] * lane[None, :] % LANES) / LANES
    last = np.concatenate(
        [np.where(imag, -np.sin(angle), np.cos(angle)), np.where(imag, np.cos(angle), np.sin(angle))], axis=1
    )
    high, low = split_host(last)
    last = np.concatenate([high, high, low], axis=1)
    return (forward_x, forward_y, inverse_y, twiddle, prop, nine, dirichlet, phase_f, phase_i, last)


def split(x):
    high = x.astype(BF16)
    low = (x - high.astype(F32)).astype(BF16)
    return high, low


def four(values, sign):
    (ar, ai), (br, bi), (cr, ci), (dr, di) = values
    s0r, s0i, s1r, s1i = ar + cr, ai + ci, ar - cr, ai - ci
    s2r, s2i, s3r, s3i = br + dr, bi + di, br - dr, bi - di
    if sign < 0:
        s3r, s3i = s3i, -s3r
        return [(s0r + s2r, s0i + s2i), (s1r + s3r, s1i + s3i), (s0r - s2r, s0i - s2i), (s1r - s3r, s1i - s3i)]
    return [(s0r + s2r, s0i + s2i), (s1r - s3i, s1i + s3r), (s0r - s2r, s0i - s2i), (s1r + s3i, s1i - s3r)]


def turn(value, power, sign):
    re, im = value
    power = power % 16
    if power == 0:
        return value
    if power == 4:
        return (im, -re) if sign < 0 else (-im, re)
    half = math.sqrt(0.5)
    if power == 2:
        if sign < 0:
            return (re + im) * half, (im - re) * half
        return (re - im) * half, (im + re) * half
    if power == 6:
        if sign < 0:
            return (im - re) * half, (re + im) * -half
        return (re + im) * -half, (re - im) * half
    c, s = math.cos(2 * math.pi * power / 16), sign * math.sin(2 * math.pi * power / 16)
    return re * c - im * s, re * s + im * c


def sixteen(values, sign):
    inner = [four([values[4 * a1 + a0] for a1 in range(4)], sign) for a0 in range(4)]
    out = [None] * 16
    for k0 in range(4):
        column = four([turn(inner[a0][k0], a0 * k0, sign) for a0 in range(4)], sign)
        for k1 in range(4):
            out[k0 + 4 * k1] = column[k1]
    return out


def cmul(ar, ai, br, bi):
    return ar * br - ai * bi, ar * bi + ai * br


def body(
    wave_count,
    pw_hbm, tr_hbm, fx_hbm, fy_hbm, iy_hbm, tw_hbm, py_hbm, nine_hbm, dk_hbm, pf_hbm, pi_hbm, last_hbm,
    pos_hbm, windex_hbm, wweight_hbm, wphase_hbm,
    out_ref,
    pos_s, windex, wweight, wphase,
    pw, tr, fx, fy, iy, tw, py, nine, dk, pf, pi, last,
    yx, send1, recv1, yy, send2, recv2, rows_re, rows_im, a_hi, a_lo, total, send3, recv3, recv_y, sum_y, back_y, recv_x, sum_x, back_x,
    load_sem, rows_sem, send1_sem, recv1_sem, send2_sem, recv2_sem, forward_sem, local_sem, send3_sem, recv3_sem, send4_sem, recv4_sem,
):
    me = lax.axis_index("row")
    wv = lax.axis_index("wave")
    share = WINDOW // wave_count

    y_lo, z, core = me // 8, lax.rem(me // 2, 4), lax.rem(me, 2)
    chip = me // 2
    sibling = 2 * chip + 1 - core

    def other_chip(n):
        return lax.rem(y_lo + n // 4, 2) * 4 + lax.rem(z + n, 4)

    def other_row(n):
        return 2 * other_chip(lax.rem(n, 8)) + lax.rem(core + n // 8, 2)

    def other_wave(n):
        return lax.rem(wv + n, 4) + lax.rem(wv // 4 + n // 4, 2) * 4

    barrier = pltpu.get_barrier_semaphore()

    def greet_row(d, _):
        pl.semaphore_signal(barrier, inc=1, device_id={"row": other_row(d)}, device_id_type=MESH)
        return 0

    def greet_wave(d, _):
        pl.semaphore_signal(barrier, inc=1, device_id={"wave": other_wave(d)}, device_id_type=MESH)
        return 0

    lax.fori_loop(1, PARTS, greet_row, 0)
    lax.fori_loop(1, wave_count, greet_wave, 0)

    tables = ((fx_hbm, fx), (tw_hbm, tw), (dk_hbm, dk), (pf_hbm, pf), (pi_hbm, pi), (fy_hbm, fy), (iy_hbm, iy),
              (py_hbm, py), (nine_hbm, nine), (last_hbm, last),
              (pos_hbm, pos_s), (windex_hbm, windex), (wweight_hbm, wweight), (wphase_hbm, wphase))
    small = [pltpu.make_async_copy(src, dst, load_sem.at[n]) for n, (src, dst) in enumerate(tables)]

    def load_rows(n):
        rows = pl.ds(n * ROWS_LOAD, ROWS_LOAD)
        return (
            pltpu.make_async_copy(pw_hbm.at[:, 0, rows], pw.at[:, rows], rows_sem.at[0, n]),
            pltpu.make_async_copy(tr_hbm.at[0, :, rows], tr.at[:, rows], rows_sem.at[1, n]),
        )

    small[1].start()
    for n in range(LANES // ROWS_LOAD):
        for load in load_rows(n):
            load.start()
    small[0].start()
    for load in small[2:]:
        load.start()
    small[1].wait()

    with jax.named_scope("column_transform"):
        def columns_16(r, _):
            rows = pl.ds(pl.multiple_of(r * 8, 8), 8)
            values = []
            for a in range(PARTS):
                cols = slice(a * LANES, (a + 1) * LANES)
                values.append(cmul(pw[0, rows, cols], pw[1, rows, cols], tr[0, rows, cols], tr[1, rows, cols]))
            for k, (re, im) in enumerate(sixteen(values, -1)):
                if k > 0:
                    re, im = cmul(re, im, tw[k, 0], tw[k, 1])
                yx[k, rows, :LANES] = re
                yx[k, rows, LANES:] = im
            return 0

        for n in range(LANES // ROWS_LOAD):
            for load in load_rows(n):
                load.wait()
            lax.fori_loop(n * ROWS_LOAD // 8, (n + 1) * ROWS_LOAD // 8, columns_16, 0)
        small[0].wait()

    pl.semaphore_wait(barrier, PARTS - 1 + wave_count - 1)

    def copy1(c, peer):
        begin, end = CHUNKS[c]
        rows = pl.ds(16 * begin, 16 * (end - begin))
        return pltpu.make_async_remote_copy(
            src_ref=send1.at[peer, rows], dst_ref=recv1.at[me, rows],
            send_sem=send1_sem.at[c, peer], recv_sem=recv1_sem.at[c, me],
            device_id={"row": peer}, device_id_type=MESH,
        )

    def arrived1(c, source):
        begin, end = CHUNKS[c]
        rows = pl.ds(16 * begin, 16 * (end - begin))
        return pltpu.make_async_remote_copy(
            src_ref=send1.at[source, rows], dst_ref=recv1.at[source, rows],
            send_sem=send1_sem.at[c, source], recv_sem=recv1_sem.at[c, source],
            device_id={"row": source}, device_id_type=MESH,
        )

    with jax.named_scope("column_products"):
        def product(j):
            high, low = split(yx[j])
            return lax.dot_general(
                fx[...], jnp.concatenate([high, low, high], axis=1), NT, preferred_element_type=F32
            )

        def columns_128(d, _):
            j = other_row(d)
            send1[j] = product(j)
            copy1(0, j).start()
            return 0

        lax.fori_loop(1, PARTS, columns_128, 0)
        for c in range(1, len(CHUNKS)):
            def more(d, _):
                copy1(c, other_row(d)).start()
                return 0

            lax.fori_loop(1, PARTS, more, 0)
        recv1[me] = product(me)

    with jax.named_scope("window_weights"):
        for load in small[2:]:
            load.wait()
        probe = lax.broadcasted_iota(jnp.int32, (PROBES, 1), 0)
        r0 = jnp.zeros((PROBES, 1), jnp.int32)
        c0 = jnp.zeros((PROBES, 1), jnp.int32)
        for p in range(PROBES):
            r0 = jnp.where(probe == p, pos_s[0, me * PROBES + p], r0)
            c0 = jnp.where(probe == p, pos_s[1, me * PROBES + p], c0)
        tilt = FACTOR * (r0 * windex[0, 0] + c0 * windex[0, 1])
        units = (2 * (c0 - HALF) + (WINDOW - 1)) * pi[...] - 2 * tilt
        units = jnp.bitwise_and(units, 2 * GRID - 1)
        angle = units.astype(F32) * (math.pi / GRID) + pf[...] + wphase[0, 0]
        rows_re[...] = jnp.cos(angle) * wweight[0, 0]
        rows_im[...] = jnp.sin(angle) * wweight[0, 0]

        def weights_of(n, _):
            p, part = n // 8, lax.rem(n, 8)
            base = dk[pl.ds(pl.multiple_of(part * 16, 16), 16), :]
            rows = pl.ds(pl.multiple_of(n * 16, 16), 16)
            re, im = rows_re[pl.ds(p, 1), :], rows_im[pl.ds(p, 1), :]
            for kind, factor in enumerate((re, re + im, im - re)):
                high, low = split(base * factor)
                a_hi[kind, rows, :] = high
                a_lo[kind, rows, :] = low
            return 0

        lax.fori_loop(0, PROBES * 8, weights_of, 0)

    def slot2(c, source):
        begin, end = CHUNKS[c]
        size = 16 * (end - begin)
        return pl.ds(pl.multiple_of(256 * begin + source * size, 16), size)

    def rows_of(c):
        begin, end = CHUNKS[c]
        return pl.ds(16 * begin, 16 * (end - begin))

    def copy2(c, block, which, target, sem):
        return pltpu.make_async_remote_copy(
            src_ref=send2.at[lax.rem(block, PARTS), rows_of(c)], dst_ref=recv2.at[which, slot2(c, me)],
            send_sem=send2_sem.at[c, sem], recv_sem=recv2_sem.at[c, which, me],
            device_id={"row": target}, device_id_type=MESH,
        )

    def copies2(c, n):
        there = other_chip(n)
        return (
            copy2(c, 2 * there, 0, 2 * there, 3 * n),
            copy2(c, 2 * there + 2, 1, 2 * there + 1, 3 * n + 1),
            copy2(c, 2 * there + 1, 1 - core, 2 * there + core, 3 * n + 2),
        )

    def copy2_sibling(c):
        return copy2(c, 2 * chip + 2 * (1 - core), 1 - core, sibling, 0)

    def forward2(c, n):
        source = 2 * other_chip(n) + core
        return pltpu.make_async_remote_copy(
            src_ref=recv2.at[1 - core, slot2(c, source)], dst_ref=recv2.at[core, slot2(c, source)],
            send_sem=forward_sem.at[c, n], recv_sem=recv2_sem.at[c, core, source],
            device_id={"row": sibling}, device_id_type=MESH,
        )

    def arrived2(c, which, source):
        return pltpu.make_async_remote_copy(
            src_ref=send2.at[source, rows_of(c)], dst_ref=recv2.at[which, slot2(c, source)],
            send_sem=send2_sem.at[c, 0], recv_sem=recv2_sem.at[c, which, source],
            device_id={"row": sibling}, device_id_type=MESH,
        )

    def keep2(c, which, block):
        return pltpu.make_async_copy(
            send2.at[lax.rem(block, PARTS), rows_of(c)], recv2.at[which, slot2(c, me)], local_sem.at[c, which]
        )

    def keeps2(c):
        return keep2(c, core, 2 * chip + 2 * core), keep2(c, 1 - core, 2 * chip + 1)

    for c, (begin, end) in enumerate(CHUNKS):
        size = 8 * (end - begin)
        with jax.named_scope("wait_columns"):
            def wait1(d, _):
                arrived1(c, other_row(d)).wait_recv()
                return 0

            lax.fori_loop(1, PARTS, wait1, 0)

        with jax.named_scope("row_transform"):
            def rows_16(g, _):
                re_rows = pl.ds(pl.multiple_of(g * 16, 8), 8)
                im_rows = pl.ds(pl.multiple_of(g * 16 + 8, 8), 8)
                here = pl.ds(pl.multiple_of((g - begin) * 8, 8), 8)
                values = [(recv1[a, re_rows, :], recv1[a, im_rows, :]) for a in range(PARTS)]
                for k, (re, im) in enumerate(sixteen(values, -1)):
                    if k > 0:
                        re, im = cmul(re, im, tw[k, 0], tw[k, 1])
                    yy[k, here, :LANES] = re
                    yy[k, here, LANES:] = im
                return 0

            lax.fori_loop(begin, end, rows_16, 0)

            kx = me + 16 * (FIRST + 8 * begin + lax.broadcasted_iota(jnp.int32, (1, size, LANES), 1))
            limit = GRID * GRID - 9 * kx * kx

            def products(n, _):
                ks = pl.ds(n * 4, 4)
                y = yy[ks, :size, :].reshape(4 * size, 2 * LANES)
                high, low = split(y)
                f = jnp.dot(jnp.concatenate([high, low, high], axis=1), fy[...], preferred_element_type=F32)
                f = f.reshape(4, size, 2 * LANES)
                re, im = cmul(f[:, :, :LANES], f[:, :, LANES:], py[ks, 0:1, :], py[ks, 1:2, :])
                open_ = nine[ks] <= limit
                re = jnp.where(open_, re, 0.0)
                im = jnp.where(open_, im, 0.0)
                f = jnp.concatenate([re, im], axis=2).reshape(4 * size, 2 * LANES)
                high, low = split(f)
                f = jnp.dot(jnp.concatenate([high, low, high], axis=1), iy[...], preferred_element_type=F32)
                yy[ks, :size, :] = f.reshape(4, size, 2 * LANES)
                return 0

            lax.fori_loop(0, 4, products, 0)

            def rows_back(g, _):
                re_rows = pl.ds(pl.multiple_of(g * 16, 8), 8)
                im_rows = pl.ds(pl.multiple_of(g * 16 + 8, 8), 8)
                here = pl.ds(pl.multiple_of((g - begin) * 8, 8), 8)
                values = []
                for k in range(PARTS):
                    re, im = yy[k, here, :LANES], yy[k, here, LANES:]
                    if k > 0:
                        re, im = cmul(re, im, tw[k, 0], -tw[k, 1])
                    values.append((re, im))
                for a, (re, im) in enumerate(sixteen(values, 1)):
                    send2[a, re_rows, :] = re
                    send2[a, im_rows, :] = im
                return 0

            lax.fori_loop(begin, end, rows_back, 0)

        with jax.named_scope("send_rows"):
            def send(n, _):
                for copy in copies2(c, n):
                    copy.start()
                return 0

            lax.fori_loop(1, PARTS // 2, send, 0)
            copy2_sibling(c).start()
            for copy in keeps2(c):
                copy.start()

    x, y_hi = lax.rem(wv, 4), wv // 4
    n_y, n_x = ROUTED
    n_d = PROBES - n_y - n_x

    def wave_of(step_y, step_x):
        return lax.rem(y_hi + step_y, 2) * 4 + lax.rem(x + step_x, 4)

    def copy_y(_):
        far = 1 - y_hi
        return pltpu.make_async_remote_copy(
            src_ref=send3.at[far, :, pl.ds(0, n_y)], dst_ref=recv_y,
            send_sem=send4_sem.at[0], recv_sem=recv4_sem.at[0],
            device_id={"wave": wave_of(1, 0)}, device_id_type=MESH,
        )

    def copy_y_back(n):
        to = lax.rem(x + n, 4)
        return pltpu.make_async_remote_copy(
            src_ref=sum_y.at[to], dst_ref=back_y.at[3 - n],
            send_sem=send4_sem.at[n], recv_sem=recv4_sem.at[4 - n],
            device_id={"wave": wave_of(0, n)}, device_id_type=MESH,
        )

    def copy_x(n):
        to = lax.rem(x + n, 4)
        return pltpu.make_async_remote_copy(
            src_ref=send3.at[:, to, pl.ds(n_y, n_x)], dst_ref=recv_x.at[3 - n],
            send_sem=send4_sem.at[3 + n], recv_sem=recv4_sem.at[7 - n],
            device_id={"wave": wave_of(0, n)}, device_id_type=MESH,
        )

    def copy_x_back(_):
        far = 1 - y_hi
        return pltpu.make_async_remote_copy(
            src_ref=sum_x.at[far], dst_ref=back_x,
            send_sem=send4_sem.at[7], recv_sem=recv4_sem.at[7],
            device_id={"wave": wave_of(1, 0)}, device_id_type=MESH,
        )

    def copy_d(n):
        to_y, to_x = lax.rem(y_hi + n // 4, 2), lax.rem(x + n, 4)
        slot = 4 * (n // 4) + lax.rem(4 - lax.rem(n, 4), 4)
        return pltpu.make_async_remote_copy(
            src_ref=send3.at[to_y, to_x, pl.ds(n_y + n_x, n_d)], dst_ref=recv3.at[slot],
            send_sem=send3_sem.at[n], recv_sem=recv3_sem.at[slot],
            device_id={"wave": wave_of(n // 4, n)}, device_id_type=MESH,
        )

    for c, (begin, end) in enumerate(CHUNKS):
        with jax.named_scope("wait_rows"):
            for copy in keeps2(c):
                copy.wait()
            forward2(c, 0).start()

            def shared(n, _):
                arrived2(c, 1 - core, 2 * other_chip(n) + core).wait_recv()
                forward2(c, n).start()
                return 0

            def exclusive(n, _):
                arrived2(c, core, other_row(n)).wait_recv()
                return 0

            def forwarded(n, _):
                arrived2(c, 1 - core, 2 * other_chip(n) + 1 - core).wait_recv()
                return 0

            lax.fori_loop(1, PARTS // 2, shared, 0)
            lax.fori_loop(1, PARTS, exclusive, 0)
            lax.fori_loop(0, PARTS // 2, forwarded, 0)
        with jax.named_scope("window_columns"):
            deep = slice(128 * begin, 128 * end)
            y = jnp.concatenate(
                [recv2[0, 256 * begin:256 * end, :], recv2[1, 256 * begin:256 * end, :]], axis=1
            ).reshape(16 * (end - begin), 2, 8, 2 * LANES)
            size = 128 * (end - begin)
            y_re, y_im = y[:, 0].reshape(size, 2 * LANES), y[:, 1].reshape(size, 2 * LANES)
            stacks = []
            for part in (y_re + y_im, y_im, y_re):
                high, low = split(part)
                stacks.append(jnp.concatenate([high, low, high], axis=0))

            def contract(b):
                rows = pl.ds(pl.multiple_of(b * BATCH * WINDOW, 16), BATCH * WINDOW)
                sums = []
                for kind in range(3):
                    high = a_hi[kind, rows, deep]
                    both = jnp.concatenate([high, high, a_lo[kind, rows, deep]], axis=1)
                    sums.append(jnp.dot(both, stacks[kind], preferred_element_type=F32))
                re, im = sums[0] - sums[1], sums[0] + sums[2]
                if c > 0:
                    re, im = re + total[0, rows, :], im + total[1, rows, :]
                return rows, re, im

            def partial(b, _):
                rows, re, im = contract(b)
                total[0, rows, :] = re
                total[1, rows, :] = im
                return 0

            if c < len(CHUNKS) - 1:
                lax.fori_loop(0, PROBES // BATCH, partial, 0)
                continue

            lane = lax.broadcasted_iota(jnp.int32, (1, LANES), 1)

            def batch(b, _):
                _, re, im = contract(b)
                for n in range(BATCH):
                    p = b * BATCH + n
                    offset = pos_s[0, me * PROBES + p] - me * LANES
                    here = slice(n * WINDOW, (n + 1) * WINDOW)
                    u = jnp.concatenate(
                        [jnp.where(lane >= offset, t[here, :LANES], t[here, LANES:]) for t in (re, im)], axis=1
                    )
                    u_high, u_low = split(u)
                    v = lax.dot_general(
                        last[...], jnp.concatenate([u_high, u_low, u_high], axis=1), NT, preferred_element_type=F32
                    )
                    send3[:, :, p] = v.reshape(2, 4, 2 * share, LANES)
                return 0

            lax.fori_loop(0, n_y // BATCH, batch, 0)
            copy_y(0).start()
            lax.fori_loop(n_y // BATCH, (n_y + n_x) // BATCH, batch, 0)
            for n in (1, 3, 2):
                copy_x(n).start()
            lax.fori_loop((n_y + n_x) // BATCH, PROBES // BATCH, batch, 0)
            for n in WAVE_ORDER:
                copy_d(n).start()

    with jax.named_scope("first_sums"):
        copy_y(0).wait_recv()
        sum_y[...] = send3[y_hi, :, :n_y] + recv_y[...]
        for n in (1, 3, 2):
            copy_y_back(n).start()
        for n in (1, 3, 2):
            copy_x(n).wait_recv()
        sum_x[...] = send3[:, x, n_y:n_y + n_x] + recv_x[0] + recv_x[1] + recv_x[2]
        copy_x_back(0).start()

    with jax.named_scope("drain"):
        def drain1(n, _):
            for c in range(len(CHUNKS)):
                copy1(c, other_row(n)).wait_send()
            return 0

        def drain2(n, _):
            for c in range(len(CHUNKS)):
                for copy in copies2(c, n):
                    copy.wait_send()
                forward2(c, n).wait_send()
            return 0

        lax.fori_loop(1, PARTS, drain1, 0)
        lax.fori_loop(1, PARTS // 2, drain2, 0)
        for c in range(len(CHUNKS)):
            copy2_sibling(c).wait_send()
            forward2(c, 0).wait_send()

        for n in (1, 2, 3):
            copy_x(n).wait_send()
            copy_y_back(n).wait_send()
        copy_y(0).wait_send()
        for n in WAVE_ORDER:
            copy_d(n).wait_send()
        copy_x_back(0).wait_send()

    with jax.named_scope("add_waves"):
        def store(first, v):
            re, im = v[:, :share], v[:, share:]
            out_ref[first:first + v.shape[0]] = (re * re + im * im) * (1.0 / (WINDOW * WINDOW * wave_count))

        for n in WAVE_ORDER:
            copy_d(n).wait_recv()
        v = send3[y_hi, x, n_y + n_x:]
        for n in WAVE_ORDER:
            v = v + recv3[n]
        store(n_y + n_x, v)
        v = sum_y[x]
        for n in (1, 2, 3):
            copy_y_back(n).wait_recv()
        store(0, v + back_y[0] + back_y[1] + back_y[2])
        copy_x_back(0).wait_recv()
        store(n_y, sum_x[y_hi] + back_x[...])


def shards(wave_count, plane_waves, transmission, wave_index, wave_weight, wave_phase, probe_pos):
    tables = [jnp.asarray(t) for t in host_tables(wave_count)]
    share = WINDOW // wave_count
    rows = plane_waves.shape[2]
    chunks = len(CHUNKS)
    largest = max(8 * (end - begin) for begin, end in CHUNKS)
    any_ = pl.BlockSpec(memory_space=pl.ANY)
    vmem = pl.BlockSpec(memory_space=pltpu.VMEM)
    return pl.pallas_call(
        functools.partial(body, wave_count),
        out_shape=jax.ShapeDtypeStruct((PROBES, share, LANES), F32),
        in_specs=[any_] * 16,
        out_specs=vmem,
        scratch_shapes=[
            pltpu.SMEM((2, PARTS * PROBES), jnp.int32),
            pltpu.SMEM((1, 2), jnp.int32),
            pltpu.SMEM((1, 1), F32),
            pltpu.SMEM((1, 1), F32),
            pltpu.VMEM((2, rows, GRID), F32),
            pltpu.VMEM((2, rows, GRID), F32),
        ]
        + [pltpu.VMEM(t.shape, t.dtype) for t in tables]
        + [
            pltpu.VMEM((PARTS, LANES, 2 * LANES), F32),
            pltpu.VMEM((PARTS, BLOCK, LANES), F32),
            pltpu.VMEM((PARTS, BLOCK, LANES), F32),
            pltpu.VMEM((PARTS, largest, 2 * LANES), F32),
            pltpu.VMEM((PARTS, BLOCK, LANES), F32),
            pltpu.VMEM((2, DEPTH, LANES), F32),
            pltpu.VMEM((PROBES, DEPTH // 2), F32),
            pltpu.VMEM((PROBES, DEPTH // 2), F32),
            pltpu.VMEM((3, PROBES * WINDOW, DEPTH // 2), BF16),
            pltpu.VMEM((3, PROBES * WINDOW, DEPTH // 2), BF16),
            pltpu.VMEM((2, PROBES * WINDOW, 2 * LANES), F32),
            pltpu.VMEM((2, 4, PROBES, 2 * share, LANES), F32),
            pltpu.VMEM((wave_count, PROBES - sum(ROUTED), 2 * share, LANES), F32),
            pltpu.VMEM((4, ROUTED[0], 2 * share, LANES), F32),
            pltpu.VMEM((4, ROUTED[0], 2 * share, LANES), F32),
            pltpu.VMEM((3, ROUTED[0], 2 * share, LANES), F32),
            pltpu.VMEM((3, 2, ROUTED[1], 2 * share, LANES), F32),
            pltpu.VMEM((2, ROUTED[1], 2 * share, LANES), F32),
            pltpu.VMEM((ROUTED[1], 2 * share, LANES), F32),
            pltpu.SemaphoreType.DMA((len(tables) + 4,)),
            pltpu.SemaphoreType.DMA((2, LANES // ROWS_LOAD)),
            pltpu.SemaphoreType.DMA((chunks, PARTS)),
            pltpu.SemaphoreType.DMA((chunks, PARTS)),
            pltpu.SemaphoreType.DMA((chunks, 3 * PARTS // 2)),
            pltpu.SemaphoreType.DMA((chunks, 2, PARTS)),
            pltpu.SemaphoreType.DMA((chunks, PARTS // 2)),
            pltpu.SemaphoreType.DMA((chunks, 2)),
            pltpu.SemaphoreType.DMA((wave_count,)),
            pltpu.SemaphoreType.DMA((wave_count,)),
            pltpu.SemaphoreType.DMA((8,)),
            pltpu.SemaphoreType.DMA((8,)),
        ],
        compiler_params=pltpu.CompilerParams(
            collective_id=0, has_side_effects=True, vmem_limit_bytes=60 * 1024 * 1024
        ),
    )(plane_waves, transmission, *tables, probe_pos.T, wave_index, wave_weight.reshape(1, 1), wave_phase.reshape(1, 1))


def solution(mesh):
    return jax.shard_map(
        functools.partial(shards, mesh.shape["wave"]),
        mesh=mesh,
        in_specs=(
            P(None, "wave", "row", None),
            P(None, None, "row", None),
            P("wave", None),
            P("wave"),
            P("wave"),
            P(),
        ),
        out_specs=P("row", "wave", None),
        check_vma=False,
    )
```
